256 devices in a mesh: dp: 16 (over x_lo, y, core), expert: 16 (over z, x_hi).
Axes of the slice: x: 4 (x_hi: 2, x_lo: 2; x = x_hi * 2 + x_lo), y: 4, z: 8, core: 2. Of those that a mesh axis runs over, the one named last changes fastest.
Arguments:
- tokens: bfloat16 [8192, 4096], P(('dp', 'expert')), may hold values from -6 to 6
- assign: int32 [256, 32], P(('dp', 'expert')), may hold values from 0 to 31, each once within a row
- w_in: bfloat16 [16, 4096, 4096], P('expert', None, 'dp'), may hold values from -0.09375 to 0.09375
- w_out: bfloat16 [16, 4096, 4096], P('expert', 'dp'), may hold values from -0.09375 to 0.09375
- cotangent: bfloat16 [8192, 4096], P(('dp', 'expert')), may hold values from -6 to 6
Outputs:
- output: bfloat16 [8192, 4096], P(('dp', 'expert'))
- grad_tokens: bfloat16 [8192, 4096], P(('dp', 'expert'))
- grad_in: bfloat16 [16, 4096, 4096], P('expert', None, 'dp')
- grad_out: bfloat16 [16, 4096, 4096], P('expert', 'dp')
The draws below stay inside these ranges and needn't reach their ends.
Inputs may be any that keep to these rules, and one draw needn't show every extreme that they name: Each row of assign is a permutation of 0 .. 31.
All inputs are finite; a program needn't handle non-finite values.
Results may differ from the reference program's by a relative error of at most 0.0049.
Values may be sent and summed in bfloat16 or wider, within the bound.
A program may use at most 128 MiB of HBM per device.

```python
import jax
import jax.numpy as jnp
from jax import lax

D = 4096
H = 4096
ROWS = 2
EXPERTS = 16
TOK_DEV = 32
SHARDS = 256
TOKENS = 8192


def block_levels(stream_key, dims, cuts, low, largest):
    loudness, own = 1.0, jax.random.fold_in(stream_key, 6)
    for dim, parts in cuts:
        draws = jnp.exp(jax.random.uniform(jax.random.fold_in(own, dim), (parts,), jnp.float32, low / len(cuts), largest / len(cuts)))
        loudness = loudness * jnp.repeat(draws, dims[dim] // parts).reshape([-1 if axis == dim else 1 for axis in range(len(dims))])
    return loudness


def centred(own_key, dims, deviation, reach, split=(), kind=jnp.bfloat16):
    level = block_levels(own_key, dims, split, -0.22, 0.18) if split else 1.0
    drawn = jax.random.normal(own_key, dims, jnp.float32) * deviation * level
    return jnp.minimum(jnp.maximum(drawn, -reach), reach).astype(kind)


def setup_inputs(seed: int = 0) -> dict:
    seeds = jax.random.split(jax.random.key(seed), 6)
    tokens = centred(seeds[0], (TOKENS, D), 1.0, 6.0, ((0, 256),))
    assign = jax.vmap(lambda own: jax.random.permutation(own, TOK_DEV))(jax.random.split(seeds[1], SHARDS)).reshape((SHARDS, TOK_DEV)).astype(jnp.int32)
    w_in = centred(seeds[2], (EXPERTS, D, H), D ** -0.5, 0.09375, ((0, 16), (2, 16)))
    w_out = centred(seeds[3], (EXPERTS, H, D), H ** -0.5, 0.09375, ((0, 16), (1, 16)))
    cotangent = centred(seeds[4], (TOKENS, D), 1.0, 6.0, ((0, 256),))
    return {"tokens": tokens, "assign": assign, "w_in": w_in, "w_out": w_out, "cotangent": cotangent}


def silu_slope(value):
    sig = jax.nn.sigmoid(value)
    return sig * (1.0 + value * (1.0 - sig))


def one_expert(items):
    rows_x, rows_g, weight_in, weight_out = items
    pre = jnp.dot(rows_x, weight_in, preferred_element_type=jnp.float32)
    act = jax.nn.silu(pre).astype(jnp.bfloat16)
    out_rows = jnp.dot(act, weight_out, preferred_element_type=jnp.float32).astype(jnp.bfloat16)
    dact = jnp.dot(rows_g, weight_out.T, preferred_element_type=jnp.float32)
    dpre = (dact * silu_slope(pre)).astype(jnp.bfloat16)
    dx_rows = jnp.dot(dpre, weight_in.T, preferred_element_type=jnp.float32).astype(jnp.bfloat16)
    grad_w_in = jnp.dot(rows_x.T, dpre, preferred_element_type=jnp.float32).astype(jnp.bfloat16)
    grad_w_out = jnp.dot(act.T, rows_g, preferred_element_type=jnp.float32).astype(jnp.bfloat16)
    return out_rows, dx_rows, grad_w_in, grad_w_out


def to_experts(values, assign):
    shaped = values.reshape(SHARDS, TOK_DEV, D)
    dealt = jnp.take_along_axis(shaped, assign.astype(jnp.int32)[:, :, None], axis=1)
    return dealt.reshape(SHARDS, EXPERTS, ROWS, D).transpose(1, 0, 2, 3).reshape(EXPERTS, SHARDS * ROWS, D)


def from_experts(values, assign):
    dealt = values.reshape(EXPERTS, SHARDS, ROWS, D).transpose(1, 0, 2, 3).reshape(SHARDS, TOK_DEV, D)

    def place(order, rows):
        return jnp.zeros_like(rows).at[order].set(rows)

    return jax.vmap(place)(assign.astype(jnp.int32), dealt).reshape(TOKENS, D)


def reference(tokens, assign, w_in, w_out, cotangent):
    rows_x = to_experts(tokens, assign)
    rows_g = to_experts(cotangent, assign)
    out_rows, dx_rows, grad_in, grad_out = lax.map(one_expert, (rows_x, rows_g, w_in, w_out))
    return from_experts(out_rows, assign), from_experts(dx_rows, assign), grad_in, grad_out
```

```python
import jax
import jax.numpy as jnp
from jax import lax
from jax.experimental import pallas as pl
from jax.experimental.pallas import tpu as pltpu
from jax.sharding import PartitionSpec as P

MESH = pl.DeviceIdType.MESH
D = 4096
HID = 256
TILE = 512
FOLD = 8
PART = 1024
EXPERTS = 16
SLOTS = [(dz, f) for dz in (0, 1, 7, 2, 6, 3, 5, 4) for f in (0, 1)]


def kernel(
    q_ref, tok_ref, cot_ref, win_hbm, wout_hbm,
    out_ref, dtok_ref, gin_hbm, gout_hbm,
    stack, a_send, a_recv, r_send, r_recv,
    xg, gg, win, wout, py, pd, sby, sbd,
    rhy, rfy, rxy, rhd, rfd, rxd,
    act, dpre, acc_a, acc_b, gin, gout,
    ssem, rsem, lsem,
):
    me = lax.axis_index("dp")
    ex = lax.axis_index("expert")
    xl, y, core = me // 8, (me // 2) % 4, me % 2
    z, xh = ex // 2, ex % 2

    def dev(xl, y, core):
        return xl * 8 + y * 2 + core

    y_up = (dev(xl, (y + 1) % 4, core), ex)
    y_dn = (dev(xl, (y + 3) % 4, core), ex)
    x_nb = (dev(1 - xl, y, core), ex)
    twin = (dev(xl, y, 1 - core), ex)

    def slot_peer(dz, f):
        xl2 = (1 - xl) if f else xl
        xh2 = (1 - xh) if f else xh
        return (dev(xl2, y, core), ((z + dz) % 8) * 2 + xh2)

    bar = pltpu.get_barrier_semaphore()
    everyone = [y_up, y_dn, x_nb, twin] + [slot_peer(*s) for s in SLOTS[1:]]
    for peer in everyone:
        pl.semaphore_signal(bar, inc=1, device_id=peer, device_id_type=MESH)

    w1 = pltpu.make_async_copy(win_hbm.at[0], win, lsem.at[0])
    w2 = pltpu.make_async_copy(wout_hbm.at[0], wout, lsem.at[1])
    w1.start()
    w2.start()

    count = [0]
    started = []

    def remote(src, dst, peer):
        i = count[0]
        count[0] += 1
        copy = pltpu.make_async_remote_copy(
            src_ref=src, dst_ref=dst, send_sem=ssem.at[i], recv_sem=rsem.at[i],
            device_id=peer, device_id_type=MESH,
        )
        copy.start()
        started.append(copy)
        return copy

    def dot(a, b):
        return jnp.dot(a, b, preferred_element_type=jnp.float32)

    def dot_t(a, b):
        return lax.dot_general(a, b, (((1,), (1,)), ((), ())), preferred_element_type=jnp.float32)

    def dot_l(a, b):
        return lax.dot_general(a, b, (((0,), (0,)), ((), ())), preferred_element_type=jnp.float32)

    for c in range(4):
        stack[pl.ds(c * 32, 32), :] = tok_ref[:, pl.ds(c * PART, PART)]
        stack[pl.ds(128 + c * 32, 32), :] = cot_ref[:, pl.ds(c * PART, PART)]
    a_send[...] = dot(q_ref[...], stack[...]).astype(jnp.bfloat16).reshape(EXPERTS, 16, PART)
    a_recv[0] = a_send[ex]

    pl.semaphore_wait(bar, len(everyone))

    deal = [None]
    for j, s in enumerate(SLOTS):
        if j:
            peer = slot_peer(*s)
            deal.append(remote(a_send.at[peer[1]], a_recv.at[j], peer))

    o = lax.broadcasted_iota(jnp.int32, (128, 128), 0)
    i = lax.broadcasted_iota(jnp.int32, (128, 128), 1)
    same = (o // 16 == i % 8) & ((o % 16) // 2 == i // 16) & (o % 2 == (i % 16) // 8)
    unfold = jnp.where(same, 1.0, 0.0).astype(jnp.bfloat16)

    def rows(k, s, dx, dy):
        return pl.ds(k * 256 + s * 128 + (dx * 4 + dy) * 16, 16)

    def arrive(k):
        for j in range(8 * k, 8 * k + 8):
            if j:
                deal[j].wait_recv()
        flat = a_recv[pl.ds(8 * k, 8)].reshape(128, PART)
        flat = dot(unfold, flat).astype(jnp.bfloat16)
        for c in range(4):
            xg[rows(k, 0, 0, 0), pl.ds(c * PART, PART)] = flat[c * 16:(c + 1) * 16]
            gg[rows(k, 0, 0, 0), pl.ds(c * PART, PART)] = flat[64 + c * 16:64 + (c + 1) * 16]

    HALF = (pl.ds(0, 2048), pl.ds(2048, 2048))

    class Gather:
        def __init__(self, k):
            self.k = k
            self.got = {}
            self.twins = []

        def send(self, ref, name, src, dst, peer, half=None):
            a, b = rows(self.k, 0, *src), rows(self.k, 0, *dst)
            if half is None:
                copy = remote(ref.at[a, :], ref.at[b, :], peer)
            else:
                copy = remote(ref.at[a, HALF[half]], ref.at[b, HALF[half]], peer)
            self.got[name, dst, half] = copy

        def wait(self, name, dst, half=None):
            self.got[name, dst, half].wait_recv()

        def share(self, ref, pos):
            a, b = rows(self.k, 0, *pos), rows(self.k, 1, *pos)
            self.twins.append(remote(ref.at[a, :], ref.at[b, :], twin))

        def spread(self, ref, name, dx):
            self.send(ref, name, (dx, 0), (dx, 3), y_up)
            self.send(ref, name, (dx, 0), (dx, 1), y_dn)

        def relay(self, ref, name, dx, dy):
            self.wait(name, (dx, dy))
            if dy == 3:
                self.send(ref, name, (dx, 3), (dx, 2), y_up, 0)
            else:
                self.send(ref, name, (dx, 1), (dx, 2), y_dn, 1)

        def cross(self, dy):
            self.send(gg, "g", (0, dy), (1, dy), x_nb)

        def e0(self):
            self.send(xg, "x", (0, 0), (1, 0), x_nb)
            self.spread(gg, "g", 0)
            self.cross(0)
            self.spread(xg, "x", 0)
            self.share(xg, (0, 0))
            self.share(gg, (0, 0))

        def e1(self):
            self.wait("x", (1, 0))
            self.spread(xg, "x", 1)
            self.share(xg, (1, 0))
            for dy in (3, 1):
                self.relay(gg, "g", 0, dy)
                self.cross(dy)
                self.share(gg, (0, dy))

        def e2(self):
            for dy in (3, 1):
                self.relay(xg, "x", 0, dy)
                self.share(xg, (0, dy))
            self.wait("g", (1, 0))
            self.share(gg, (1, 0))

        def e3(self):
            for dy in (3, 1):
                self.relay(xg, "x", 1, dy)
                self.share(xg, (1, dy))

        def e4(self):
            self.wait("g", (0, 2), 0)
            self.wait("g", (0, 2), 1)
            self.cross(2)
            self.share(gg, (0, 2))

        def e5(self):
            self.wait("g", (1, 3))
            self.share(gg, (1, 3))
            self.wait("x", (0, 2), 0)
            self.wait("x", (0, 2), 1)
            self.share(xg, (0, 2))
            self.wait("g", (1, 1))
            self.share(gg, (1, 1))
            self.wait("x", (1, 2), 0)
            self.wait("x", (1, 2), 1)
            self.share(xg, (1, 2))
            self.wait("g", (1, 2))
            self.share(gg, (1, 2))

        def e6(self):
            for copy in self.twins:
                copy.wait_recv()

    def chunk(k):
        return pl.ds(k * 256, 256)

    def hidden(k):
        acc_a[...] = jnp.zeros_like(acc_a)
        acc_b[...] = jnp.zeros_like(acc_b)

        @pl.loop(0, D // PART)
        def _(n):
            cols = pl.ds(pl.multiple_of(n * PART, PART), PART)
            acc_a[...] += dot(xg[chunk(k), cols], win[cols, :])
            acc_b[...] += dot_t(gg[chunk(k), cols], wout[:, cols])

        pre = acc_a[...]
        sig = jax.nn.sigmoid(pre)
        act[chunk(k), :] = (pre * sig).astype(jnp.bfloat16)
        dpre[chunk(k), :] = (acc_b[...] * (sig * (1.0 + pre * (1.0 - sig)))).astype(jnp.bfloat16)

    def add(ref, at, *others):
        total = ref[at].astype(jnp.float32)
        for other, where in others:
            total = total + other[where].astype(jnp.float32)
        ref[at] = total.astype(jnp.bfloat16)

    class Reduce:
        def __init__(self, k):
            self.k = k
            self.y2 = []
            self.d2 = []
            self.c = {}

        def pair(self, p, sb, h):
            far = pl.ds(self.k * 256 + 128, 128)
            return remote(p.at[far, HALF[h]], sb.at[pl.ds(self.k * 128, 128), HALF[h]], twin)

        def make_y(self):
            a = act[chunk(self.k), :]
            for h in range(2):

                @pl.loop(0, 4)
                def _(n):
                    cols = pl.ds(pl.multiple_of(h * 2048 + n * TILE, TILE), TILE)
                    py[chunk(self.k), cols] = dot(act[chunk(self.k), :], wout[:, cols]).astype(jnp.bfloat16)

                self.y2.append(self.pair(py, sby, h))

        def make_d(self):
            for h in range(2):

                @pl.loop(0, 4)
                def _(n):
                    cols = pl.ds(pl.multiple_of(h * 2048 + n * TILE, TILE), TILE)
                    pd[chunk(self.k), cols] = dot_t(dpre[chunk(self.k), :], win[cols, :]).astype(jnp.bfloat16)

                self.d2.append(self.pair(pd, sbd, h))

        def fold(self, p, sb, copies):
            for h in range(2):
                copies[h].wait_recv()

                @pl.loop(0, 4)
                def _(n):
                    cols = pl.ds(pl.multiple_of(h * 2048 + n * TILE, TILE), TILE)
                    add(p, (pl.ds(self.k * 256, 128), cols), (sb, (pl.ds(self.k * 128, 128), cols)))

        def at(self, dx, dy):
            return rows(self.k, 0, dx, dy)

        def far(self, p, rh, name, dx):
            src = self.at(dx, 2)
            for h, peer in ((0, y_up), (1, y_dn)):
                self.c[name, "h", dx, h] = remote(p.at[src, HALF[h]], rh.at[self.k, dx, :, HALF[h]], peer)

        def near(self, p, rh, rf, name, dx):
            for h, dy, peer in ((0, 1, y_up), (1, 3, y_dn)):
                self.c[name, "h", dx, h].wait_recv()
                at = self.at(dx, dy)
                add(p, (at, HALF[h]), (rh, (self.k, dx, slice(None), HALF[h])))
                self.c[name, "f", dx, h] = remote(p.at[at, :], rf.at[self.k, dx, h], peer)

        def own(self, p, rf, name, dx):
            for h in range(2):
                self.c[name, "f", dx, h].wait_recv()
            add(p, (self.at(dx, 0), slice(None)), (rf, (self.k, dx, 0)), (rf, (self.k, dx, 1)))

        def s3(self):
            self.fold(py, sby, self.y2)
            self.far(py, rhy, "y", 1)
            self.far(py, rhy, "y", 0)

        def s4(self):
            self.fold(pd, sbd, self.d2)
            for dy in (2, 1, 3, 0):
                self.c["d", "x", dy] = remote(pd.at[self.at(1, dy), :], rxd.at[self.k, dy], x_nb)

        def s5(self):
            self.near(py, rhy, rfy, "y", 1)
            self.near(py, rhy, rfy, "y", 0)

        def s6(self):
            for dy in (2, 1, 3, 0):
                self.c["d", "x", dy].wait_recv()
                add(pd, (self.at(0, dy), slice(None)), (rxd, (self.k, dy)))
                if dy == 2:
                    self.far(pd, rhd, "d", 0)

        def s7(self):
            self.own(py, rfy, "y", 1)
            self.c["y", "x"] = remote(py.at[self.at(1, 0), :], rxy.at[self.k], x_nb)
            self.own(py, rfy, "y", 0)

        def s8(self):
            self.near(pd, rhd, rfd, "d", 0)

        def s9(self):
            self.c["y", "x"].wait_recv()
            add(py, (self.at(0, 0), slice(None)), (rxy, (self.k,)))

        def s10(self):
            self.own(pd, rfd, "d", 0)

        def s11(self):
            at = self.at(0, 0)
            parts = [py[at, pl.ds(c * PART, PART)] for c in range(4)]
            parts += [pd[at, pl.ds(c * PART, PART)] for c in range(4)]
            flat = dot_l(unfold, jnp.concatenate(parts, axis=0)).astype(jnp.bfloat16)
            r_send[pl.ds(8 * self.k, 8)] = flat.reshape(8, 16, PART)
            if self.k == 0:
                r_recv[ex] = r_send[0]
            self.back = []
            for j in range(8 * self.k, 8 * self.k + 8):
                if j:
                    dz, f = SLOTS[j]
                    peer = slot_peer(8 - dz, f)
                    self.back.append(remote(r_send.at[j], r_recv.at[ex], peer))

    def grad_out(part):
        @pl.loop(0, 2)
        def _(n):
            cols = pl.ds(pl.multiple_of(part * 1024 + n * TILE, TILE), TILE)
            gout[:, cols] = dot_l(act[...], gg[:, cols]).astype(jnp.bfloat16)

    def grad_in(part):
        @pl.loop(0, 2)
        def _(n):
            cols = pl.ds(pl.multiple_of(part * 1024 + n * TILE, TILE), TILE)
            gin[cols, :] = dot_l(xg[:, cols], dpre[...]).astype(jnp.bfloat16)

    g0, g1 = Gather(0), Gather(1)
    r0, r1 = Reduce(0), Reduce(1)
    arrive(0)
    g0.e0()
    g0.e1()
    g0.e2()
    arrive(1)
    g0.e3()
    g1.e0()
    g0.e4()
    g0.e5()
    g1.e1()
    w1.wait()
    w2.wait()
    g0.e6()
    hidden(0)
    g1.e2()
    r0.make_y()
    g1.e3()
    r0.make_d()
    r0.s3()
    g1.e4()
    r0.s4()
    r0.s5()
    g1.e5()
    r0.s6()
    g1.e6()
    hidden(1)
    r0.s7()
    r0.s8()
    r1.make_y()
    r0.s9()
    r0.s10()
    r1.make_d()
    r1.s3()
    r0.s11()
    r1.s4()
    grad_out(0)
    grad_out(1)
    r1.s5()
    grad_out(2)
    r1.s6()
    grad_out(3)
    wo = pltpu.make_async_copy(gout, gout_hbm.at[0], lsem.at[2])
    wo.start()
    r1.s7()
    grad_in(0)
    r1.s8()
    grad_in(1)
    r1.s9()
    grad_in(2)
    r1.s10()
    r1.s11()
    grad_in(3)
    wi = pltpu.make_async_copy(gin, gin_hbm.at[0], lsem.at[3])
    wi.start()
    for copy in r0.back + r1.back:
        copy.wait_recv()
    back = dot_l(q_ref[...], r_recv[...].reshape(256, PART)).astype(jnp.bfloat16)
    for c in range(4):
        out_ref[:, pl.ds(c * PART, PART)] = back[c * 32:(c + 1) * 32]
        dtok_ref[:, pl.ds(c * PART, PART)] = back[128 + c * 32:128 + (c + 1) * 32]
    for copy in started:
        copy.wait_send()
    wo.wait()
    wi.wait()


COPIES = 2 * 15 + 2 * (17 + 16) + 2 * (4 + 8 + 9)


def body(tokens, assign, w_in, w_out, cotangent):
    bf = jnp.bfloat16
    folded = jnp.repeat(assign[0].reshape(EXPERTS, 2), FOLD, axis=1).reshape(256)
    where = jnp.tile(jnp.arange(FOLD, dtype=jnp.int32), 32) * 32 + folded
    q = (where[:, None] == jnp.arange(256, dtype=jnp.int32)[None, :]).astype(bf)

    vmem = pl.BlockSpec(memory_space=pltpu.VMEM)
    hbm = pl.BlockSpec(memory_space=pl.ANY)
    v = pltpu.VMEM
    return pl.pallas_call(
        kernel,
        out_shape=(
            jax.ShapeDtypeStruct(tokens.shape, bf),
            jax.ShapeDtypeStruct(tokens.shape, bf),
            jax.ShapeDtypeStruct(w_in.shape, bf),
            jax.ShapeDtypeStruct(w_out.shape, bf),
        ),
        in_specs=[vmem, vmem, vmem, hbm, hbm],
        out_specs=(vmem, vmem, hbm, hbm),
        scratch_shapes=[
            v((256, PART), bf),
            v((EXPERTS, 16, PART), bf), v((EXPERTS, 16, PART), bf),
            v((EXPERTS, 16, PART), bf), v((EXPERTS, 16, PART), bf),
            v((512, D), bf), v((512, D), bf),
            v((D, HID), bf), v((HID, D), bf),
            v((512, D), bf), v((512, D), bf),
            v((256, D), bf), v((256, D), bf),
            v((2, 2, 16, D), bf), v((2, 2, 2, 16, D), bf), v((2, 16, D), bf),
            v((2, 1, 16, D), bf), v((2, 1, 2, 16, D), bf), v((2, 4, 16, D), bf),
            v((512, HID), bf), v((512, HID), bf),
            v((256, HID), jnp.float32), v((256, HID), jnp.float32),
            v((D, HID), bf), v((HID, D), bf),
            pltpu.SemaphoreType.DMA((COPIES,)),
            pltpu.SemaphoreType.DMA((COPIES,)),
            pltpu.SemaphoreType.DMA((4,)),
        ],
        compiler_params=pltpu.CompilerParams(
            collective_id=0, has_side_effects=True, vmem_limit_bytes=56 * 2**20
        ),
        cost_estimate=pl.CostEstimate(
            flops=12 * 512 * D * HID, bytes_accessed=10 * 2**20, transcendentals=512 * HID
        ),
    )(q, tokens, cotangent, w_in, w_out)


def solution(mesh):
    in_specs = (
        P(("dp", "expert"), None),
        P(("dp", "expert"), None),
        P("expert", None, "dp"),
        P("expert", "dp", None),
        P(("dp", "expert"), None),
    )
    out_specs = (
        P(("dp", "expert"), None),
        P(("dp", "expert"), None),
        P("expert", None, "dp"),
        P("expert", "dp", None),
    )
    return jax.shard_map(body, mesh=mesh, in_specs=in_specs, out_specs=out_specs, check_vma=False)
```

```python
import jax
import jax.numpy as jnp
from jax import lax
from jax.experimental import pallas as pl
from jax.experimental.pallas import tpu as pltpu
from jax.sharding import PartitionSpec as P

MESH = pl.DeviceIdType.MESH
D = 4096
HID = 256
TILE = 512
PART = 1024
EXPERTS = 16
SLOTS = [(0, 0), (0, 1), (1, 0), (1, 1), (7, 0), (7, 1), (2, 0), (6, 1)]
SLOTS += [(3, 0), (3, 1), (5, 0), (5, 1), (4, 0), (4, 1), (2, 1), (6, 0)]
LOW, HIGH = (0, 2048), (2048, 2048)
FIRST, MIDDLE, LAST = (0, 1024), (1024, 2048), (3072, 1024)


class Sent:
    def __init__(self, copy):
        self.copy = copy
        self.due = True

    def wait_recv(self):
        if self.due:
            self.copy.wait_recv()
        self.due = False


def kernel(
    assign_hbm, tok_hbm, cot_hbm, win_hbm, wout_hbm,
    out_ref, dtok_ref, gin, gout,
    assign_ref, stack, a_send, a_recv, r_send, r_recv,
    xg, gg, win, wout,
    own_y, own_d, far_y, far_d, sb_y, sb_d, st_y, st_d,
    rh_y, rf_y, rx_y, rh_d, rf_d, rx_d, rq_d,
    act, dpre, acc_a, acc_b,
    ssem, rsem, lsem,
):
    bf, f32 = jnp.bfloat16, jnp.float32
    me = lax.axis_index("dp")
    ex = lax.axis_index("expert")
    xl, y, core = me // 8, (me // 2) % 4, me % 2
    z, xh = ex // 2, ex % 2

    def dev(xl, y, core):
        return xl * 8 + y * 2 + core

    y_up = (dev(xl, (y + 1) % 4, core), ex)
    y_dn = (dev(xl, (y + 3) % 4, core), ex)
    x_nb = (dev(1 - xl, y, core), ex)
    twin = (dev(xl, y, 1 - core), ex)

    def slot_peer(dz, f):
        xl2 = (1 - xl) if f else xl
        xh2 = (1 - xh) if f else xh
        return (dev(xl2, y, core), ((z + dz) % 8) * 2 + xh2)

    bar = pltpu.get_barrier_semaphore()
    everyone = [slot_peer(*s) for s in SLOTS[:0:-1]] + [y_up, y_dn, x_nb, twin]
    for peer in everyone:
        pl.semaphore_signal(bar, inc=1, device_id=peer, device_id_type=MESH)

    load = [pltpu.make_async_copy(assign_hbm, assign_ref, lsem.at[0])]
    for n in range(8):
        src = (tok_hbm, cot_hbm)[n // 4].at[:, pl.ds(n % 4 * PART, PART)]
        load.append(pltpu.make_async_copy(src, stack.at[pl.ds(n * 32, 32), :], lsem.at[1 + n]))
    w1 = pltpu.make_async_copy(win_hbm.at[0], win, lsem.at[9])
    w2 = pltpu.make_async_copy(wout_hbm.at[0], wout, lsem.at[10])
    for copy in load + [w1, w2]:
        copy.start()

    count = [0]
    started = []

    def remote(src, dst, peer):
        i = count[0]
        count[0] += 1
        copy = pltpu.make_async_remote_copy(
            src_ref=src, dst_ref=dst, send_sem=ssem.at[i], recv_sem=rsem.at[i],
            device_id=peer, device_id_type=MESH,
        )
        copy.start()
        started.append(Sent(copy))
        return started[-1]

    def dot(a, b):
        return jnp.dot(a, b, preferred_element_type=f32)

    def dot_t(a, b):
        return lax.dot_general(a, b, (((1,), (1,)), ((), ())), preferred_element_type=f32)

    def dot_l(a, b):
        return lax.dot_general(a, b, (((0,), (0,)), ((), ())), preferred_element_type=f32)

    def iota(shape, dim):
        return lax.broadcasted_iota(jnp.int32, shape, dim)

    for copy in load:
        copy.wait()
    spread = jnp.where(iota((32, 256), 0) == iota((32, 256), 1) // 8, 1.0, 0.0).astype(bf)
    order = jnp.broadcast_to(assign_ref[...].astype(f32), (16, 32)).astype(bf)
    order = dot(order, spread)[0:1, :]
    row, col = iota((256, 256), 0), iota((256, 256), 1)
    hit = ((row // 32) == (col % 8)) & ((row % 32).astype(f32) == order)
    taken = jnp.where(hit, 1.0, 0.0).astype(bf)

    a_send[...] = dot_l(taken, stack[...]).astype(bf).reshape(EXPERTS, 16, PART)
    a_recv[0] = a_send[ex]

    o, i = iota((128, 128), 0), iota((128, 128), 1)
    same = (o // 16 == i % 8) & ((o % 16) // 2 == i // 16) & (o % 2 == (i % 16) // 8)
    unfold = jnp.where(same, 1.0, 0.0).astype(bf)

    pl.semaphore_wait(bar, len(everyone))

    deal = {}

    def deal_out(k):
        for j in range(8 * k, 8 * k + 8):
            if j:
                peer = slot_peer(*SLOTS[j])
                deal[j] = remote(a_send.at[peer[1]], a_recv.at[j], peer)

    def rows(k, s, dx, dy):
        return pl.ds(k * 256 + s * 128 + (dx * 4 + dy) * 16, 16)

    def block(dx, dy):
        return pl.ds((dx * 4 + dy) * 16, 16)

    def span(cols):
        return pl.ds(*cols)

    class Gather:
        def __init__(self, k):
            self.k = k
            self.got = {}
            self.twins = {True: [], False: []}

        def send(self, ref, src, dst, peer, cols=(0, D)):
            a, b = rows(self.k, 0, *src), rows(self.k, 0, *dst)
            copy = remote(ref.at[a, span(cols)], ref.at[b, span(cols)], peer)
            self.got.setdefault((ref is xg, dst), []).append(copy)

        def wait(self, ref, dst):
            for copy in self.got[ref is xg, dst]:
                copy.wait_recv()

        def share(self, ref, pos):
            a, b = rows(self.k, 0, *pos), rows(self.k, 1, *pos)
            self.twins[ref is xg].append(remote(ref.at[a, :], ref.at[b, :], twin))

        def round_y(self, ref, dx):
            self.send(ref, (dx, 0), (dx, 3), y_up)
            self.send(ref, (dx, 0), (dx, 1), y_dn)

        def arrive(self):
            k = self.k
            for j in range(8 * k, 8 * k + 8):
                if j:
                    deal[j].wait_recv()
            flat = a_recv[pl.ds(8 * k, 8)].reshape(128, PART)
            flat = dot(unfold, flat).astype(bf)
            for c in range(4):
                xg[rows(k, 0, 0, 0), pl.ds(c * PART, PART)] = flat[c * 16:(c + 1) * 16]
                gg[rows(k, 0, 0, 0), pl.ds(c * PART, PART)] = flat[64 + c * 16:64 + (c + 1) * 16]
            self.send(xg, (0, 0), (1, 0), x_nb)
            self.round_y(gg, 0)
            self.send(gg, (0, 0), (1, 0), x_nb)
            self.round_y(xg, 0)
            self.share(xg, (0, 0))
            self.share(gg, (0, 0))

        def take(self, ref, dx, dy):
            self.wait(ref, (dx, dy))
            side = ref is gg and dx == 1
            if dy == 3:
                self.send(ref, (dx, 3), (dx, 2), y_up, FIRST if side else LOW)
            elif dy == 1:
                self.send(ref, (dx, 1), (dx, 2), y_dn, LAST if side else HIGH)
            if ref is gg and dx == 0 and dy:
                self.send(gg, (0, dy), (1, dy), x_nb, MIDDLE if dy == 2 else (0, D))
            if ref is xg and dx == 1 and dy == 0:
                self.round_y(xg, 1)
            self.share(ref, (dx, dy))

        def whole(self, ref):
            for copy in self.twins[ref is xg]:
                copy.wait_recv()

    def chunk(k):
        return pl.ds(k * 256, 256)

    def hidden_x(k):
        acc_a[...] = jnp.zeros_like(acc_a)

        @pl.loop(0, D // PART)
        def _(n):
            cols = pl.ds(pl.multiple_of(n * PART, PART), PART)
            acc_a[...] += dot(xg[chunk(k), cols], win[cols, :])

    def hidden_g(k):
        acc_b[...] = jnp.zeros_like(acc_b)

        @pl.loop(0, D // PART)
        def _(n):
            cols = pl.ds(pl.multiple_of(n * PART, PART), PART)
            acc_b[...] += dot_t(gg[chunk(k), cols], wout[:, cols])

        pre = acc_a[...]
        sig = jax.nn.sigmoid(pre)
        act[chunk(k), :] = (pre * sig).astype(bf)
        dpre[chunk(k), :] = (acc_b[...] * (sig * (1.0 + pre * (1.0 - sig)))).astype(bf)

    class Reduce:
        def __init__(self, k, own, far, sb, st, rh, rf):
            self.k, self.own, self.far, self.sb, self.st = k, own, far, sb, st
            self.rh, self.rf = rh, rf
            self.pair = []
            self.half = {}
            self.full = {}

        def make(self, h, product):
            k = self.k

            @pl.loop(0, 4)
            def _(n):
                cols = pl.ds(pl.multiple_of(h * 2048 + n * TILE, TILE), TILE)
                t = product(k, cols)
                self.own[k, :, cols] = t[:128]
                self.far[k, :, cols] = t[128:].astype(bf)

            cols = span((LOW, HIGH)[h])
            self.pair.append(remote(self.far.at[k, :, cols], self.sb.at[k, :, cols], twin))

        def total(self, dst, dx, dy, cols, *others):
            @pl.loop(0, cols[1] // PART)
            def _(n):
                at = pl.ds(pl.multiple_of(cols[0] + n * PART, PART), PART)
                t = self.own[self.k, block(dx, dy), at] + self.sb[self.k, block(dx, dy), at].astype(f32)
                for other in others:
                    t = t + other[:, at].astype(f32)
                dst[:, at] = t.astype(bf)

        def stage(self, dx, dy):
            return self.st.at[self.k, dx * 4 + dy]

        def twins(self):
            for copy in self.pair:
                copy.wait_recv()

        def send_far(self, dx):
            self.twins()
            extra = (rx_d.at[self.k, 2],) if self is d[self.k] else ()
            if extra:
                cross[self.k, 2].wait_recv()
            st = self.stage(dx, 2)
            if extra:
                self.total(st, dx, 2, FIRST)
                self.total(st, dx, 2, MIDDLE, *extra)
                self.total(st, dx, 2, LAST)
            else:
                self.total(st, dx, 2, (0, D))
            for h, cols, peer in ((0, LOW, y_up), (1, HIGH, y_dn)):
                self.half[dx, h] = remote(st.at[:, span(cols)], self.rh.at[self.k, dx, :, span(cols)], peer)

        def send_near(self, dx, h):
            dy = (1, 3)[h]
            extra = ()
            if self is d[self.k]:
                cross[self.k, dy].wait_recv()
                extra = (rx_d.at[self.k, dy],)
            self.half[dx, h].wait_recv()
            st = self.stage(dx, dy)
            self.total(st, dx, dy, (LOW, HIGH)[h], self.rh.at[self.k, dx], *extra)
            self.total(st, dx, dy, (LOW, HIGH)[1 - h], *extra)
            self.full[dx, h] = remote(st, self.rf.at[self.k, dx, h], (y_up, y_dn)[h])

        def last(self, dx, *extra):
            for h in range(2):
                self.full[dx, h].wait_recv()
            f = self.rf
            self.total(self.stage(dx, 0), dx, 0, (0, D), f.at[self.k, dx, 0], f.at[self.k, dx, 1], *extra)

    cross, side, back = {}, {}, []

    def y_product(k, cols):
        return dot(act[chunk(k), :], wout[:, cols])

    def d_product(k, cols):
        return dot_t(dpre[chunk(k), :], win[cols, :])

    def d_cross(k, dy):
        r = d[k]
        r.twins()
        st = r.stage(1, dy)
        if dy == 2:
            r.total(st, 1, 2, (0, D))
            cross[k, 2] = remote(st.at[:, span(MIDDLE)], rx_d.at[k, 2, :, span(MIDDLE)], x_nb)
            for h, cols, peer in ((0, FIRST, y_dn), (1, LAST, y_up)):
                side[k, h] = remote(st.at[:, span(cols)], rq_d.at[k, h, :, span(cols)], peer)
            return
        if dy == 0:
            r.total(st, 1, 0, (0, D))
        elif dy == 3:
            side[k, 0].wait_recv()
            r.total(st, 1, 3, FIRST, rq_d.at[k, 0])
            r.total(st, 1, 3, MIDDLE)
            r.total(st, 1, 3, LAST)
        else:
            side[k, 1].wait_recv()
            r.total(st, 1, 1, LAST, rq_d.at[k, 1])
            r.total(st, 1, 1, FIRST)
            r.total(st, 1, 1, MIDDLE)
        cross[k, dy] = remote(st, rx_d.at[k, dy], x_nb)

    def y_cross(k):
        yy[k].last(1)
        cross[k, "y"] = remote(yy[k].stage(1, 0), rx_y.at[k], x_nb)

    def y_done(k):
        cross[k, "y"].wait_recv()
        yy[k].last(0, rx_y.at[k])

    def d_done(k):
        cross[k, 0].wait_recv()
        d[k].last(0, rx_d.at[k, 0])

    def give_back(k):
        parts = [st_y[k, 0, :, pl.ds(c * PART, PART)] for c in range(4)]
        parts += [st_d[k, 0, :, pl.ds(c * PART, PART)] for c in range(4)]
        flat = dot_l(unfold, jnp.concatenate(parts, axis=0)).astype(bf)
        r_send[pl.ds(8 * k, 8)] = flat.reshape(8, 16, PART)
        if k == 0:
            r_recv[ex] = r_send[0]
        for j in range(8 * k, 8 * k + 8):
            if j:
                dz, f = SLOTS[j]
                back.append(remote(r_send.at[j], r_recv.at[ex], slot_peer(8 - dz, f)))

    def grad_out(part):
        @pl.loop(0, 2)
        def _(n):
            cols = pl.ds(pl.multiple_of(part * 1024 + n * TILE, TILE), TILE)
            gout[0, :, cols] = dot_l(act[...], gg[:, cols]).astype(bf)

    def grad_in(part):
        @pl.loop(0, 2)
        def _(n):
            cols = pl.ds(pl.multiple_of(part * 1024 + n * TILE, TILE), TILE)
            gin[0, cols, :] = dot_l(xg[:, cols], dpre[...]).astype(bf)

    def weights():
        w1.wait()
        w2.wait()

    g = [Gather(k) for k in range(2)]
    yy = [Reduce(k, own_y, far_y, sb_y, st_y, rh_y, rf_y) for k in range(2)]
    d = [Reduce(k, own_d, far_d, sb_d, st_d, rh_d, rf_d) for k in range(2)]

    step = {"w": weights}
    for k in range(2):
        for name, call in (
            ("s", lambda k: deal_out(k)),
            ("a", lambda k: g[k].arrive()),
            ("X", lambda k: g[k].whole(xg)),
            ("G", lambda k: g[k].whole(gg)),
            ("hx", hidden_x),
            ("hg", hidden_g),
            ("my0", lambda k: yy[k].make(0, y_product)),
            ("my1", lambda k: yy[k].make(1, y_product)),
            ("md0", lambda k: d[k].make(0, d_product)),
            ("md1", lambda k: d[k].make(1, d_product)),
            ("yf0", lambda k: yy[k].send_far(0)),
            ("yf1", lambda k: yy[k].send_far(1)),
            ("df", lambda k: d[k].send_far(0)),
            ("yn00", lambda k: yy[k].send_near(0, 0)),
            ("yn01", lambda k: yy[k].send_near(0, 1)),
            ("yn10", lambda k: yy[k].send_near(1, 0)),
            ("yn11", lambda k: yy[k].send_near(1, 1)),
            ("dn0", lambda k: d[k].send_near(0, 0)),
            ("dn1", lambda k: d[k].send_near(0, 1)),
            ("dx0", lambda k: d_cross(k, 0)),
            ("dx1", lambda k: d_cross(k, 1)),
            ("dx2", lambda k: d_cross(k, 2)),
            ("dx3", lambda k: d_cross(k, 3)),
            ("yx", y_cross),
            ("y", y_done),
            ("d", d_done),
            ("b", give_back),
        ):
            step[name + ".%d" % k] = (lambda call, k: lambda: call(k))(call, k)
        for ref, letter in ((xg, "x"), (gg, "g")):
            for dx in range(2):
                for dy in range(4):
                    step["%s%d%d.%d" % (letter, dx, dy, k)] = (
                        lambda k, ref, dx, dy: lambda: g[k].take(ref, dx, dy)
                    )(k, ref, dx, dy)
    for part in range(4):
        step["go%d" % part] = (lambda part: lambda: grad_out(part))(part)
        step["gi%d" % part] = (lambda part: lambda: grad_in(part))(part)

    for name in ORDER:
        step[name]()
    assert count[0] == COPIES, count[0]
    for sent in started:
        sent.wait_recv()
    home = dot(taken, r_recv[...].reshape(256, PART)).astype(bf)
    for c in range(4):
        out_ref[:, pl.ds(c * PART, PART)] = home[c * 32:(c + 1) * 32]
        dtok_ref[:, pl.ds(c * PART, PART)] = home[128 + c * 32:128 + (c + 1) * 32]
    for sent in started:
        sent.copy.wait_send()


ORDER = (
    "s.0", "s.1", "a.0", "x10.0", "g01.0", "g03.0", "x03.0", "x01.0", "x11.0", "x13.0", "g11.0", "g02.0",
    "g13.0", "a.1", "x02.0", "g10.0", "x12.0", "g12.0", "X.0", "w", "hx.0", "G.0", "hg.0", "x10.1",
    "g01.1", "md0.0", "g03.1", "md1.0", "x03.1", "my1.0", "x01.1", "my0.0", "dx2.0", "x11.1", "g11.1",
    "x13.1", "g02.1", "g10.1", "g13.1", "yf1.0", "dx1.0", "yf0.0", "x02.1", "dx3.0", "dx0.0", "df.0",
    "x12.1", "g12.1", "X.1", "hx.1", "yn11.0", "G.1", "yn10.0", "hg.1", "yn01.0", "my1.1", "dn0.0",
    "md1.1", "dn1.0", "md0.1", "yx.0", "yn00.0", "my0.1", "dx2.1", "yf1.1", "yf0.1", "dx3.1", "df.1",
    "gi2", "dx1.1", "yn11.1", "yn10.1", "yn00.1", "dn1.1", "dx0.1", "yn01.1", "d.0", "gi1", "gi3", "y.0",
    "dn0.1", "yx.1", "go0", "b.0", "go2", "d.1", "y.1", "b.1", "go3", "go1", "gi0",
)

COPIES = 2 * 15 + 2 * (19 + 16 + 23)


def body(tokens, assign, w_in, w_out, cotangent):
    bf, f32 = jnp.bfloat16, jnp.float32
    vmem = pl.BlockSpec(memory_space=pltpu.VMEM)
    hbm = pl.BlockSpec(memory_space=pltpu.HBM)
    v = pltpu.VMEM
    shapes = tuple(jax.ShapeDtypeStruct(a.shape, bf) for a in (tokens, tokens, w_in, w_out))
    return pl.pallas_call(
        kernel,
        out_shape=shapes,
        in_specs=[hbm] * 5,
        out_specs=(vmem,) * 4,
        scratch_shapes=[
            v((1, 32), jnp.int32), v((256, PART), bf),
            v((EXPERTS, 16, PART), bf), v((EXPERTS, 16, PART), bf),
            v((EXPERTS, 16, PART), bf), v((EXPERTS, 16, PART), bf),
            v((512, D), bf), v((512, D), bf),
            v((D, HID), bf), v((HID, D), bf),
            v((2, 128, D), f32), v((2, 128, D), f32),
            v((2, 128, D), bf), v((2, 128, D), bf),
            v((2, 128, D), bf), v((2, 128, D), bf),
            v((2, 8, 16, D), bf), v((2, 8, 16, D), bf),
            v((2, 2, 16, D), bf), v((2, 2, 2, 16, D), bf), v((2, 16, D), bf),
            v((2, 1, 16, D), bf), v((2, 1, 2, 16, D), bf), v((2, 4, 16, D), bf), v((2, 2, 16, D), bf),
            v((512, HID), bf), v((512, HID), bf),
            v((256, HID), f32), v((256, HID), f32),
            pltpu.SemaphoreType.DMA((COPIES,)),
            pltpu.SemaphoreType.DMA((COPIES,)),
            pltpu.SemaphoreType.DMA((11,)),
        ],
        compiler_params=pltpu.CompilerParams(
            collective_id=0, has_side_effects=True, vmem_limit_bytes=47 * 2**20
        ),
        cost_estimate=pl.CostEstimate(
            flops=12 * 512 * D * HID, bytes_accessed=10 * 2**20, transcendentals=512 * HID
        ),
    )(assign, tokens, cotangent, w_in, w_out)


def solution(mesh):
    in_specs = (
        P(("dp", "expert"), None),
        P(("dp", "expert"), None),
        P("expert", None, "dp"),
        P("expert", "dp", None),
        P(("dp", "expert"), None),
    )
    out_specs = (
        P(("dp", "expert"), None),
        P(("dp", "expert"), None),
        P("expert", None, "dp"),
        P("expert", "dp", None),
    )
    return jax.shard_map(body, mesh=mesh, in_specs=in_specs, out_specs=out_specs, check_vma=False)
```

```python
import jax
import jax.numpy as jnp
from jax import lax
from jax.experimental import pallas as pl
from jax.experimental.pallas import tpu as pltpu
from jax.sharding import PartitionSpec as P

MESH = pl.DeviceIdType.MESH
D = 4096
HID = 256
TILE = 512
PART = 512
WIDE = 1024
EXPERTS = 16
SLOTS = [(0, 0), (0, 1), (1, 0), (1, 1), (7, 0), (7, 1), (2, 0), (6, 1)]
SLOTS += [(3, 0), (3, 1), (5, 0), (5, 1), (4, 0), (4, 1), (2, 1), (6, 0)]
LOW, HIGH = (0, 2048), (2048, 2048)
FIRST, MIDDLE, LAST = (0, 1024), (1024, 2048), (3072, 1024)


class Sent:
    def __init__(self, copy):
        self.copy = copy
        self.due = True

    def wait_recv(self):
        if self.due:
            self.copy.wait_recv()
        self.due = False


def kernel(
    rows_hbm, win_hbm, wout_hbm,
    out_ref, dtok_ref, gin, gout,
    assign_ref, stack, a_send, a_recv, r_send, r_recv,
    xg, gg, win, wout,
    own_y, own_d, far_y, far_d, sb_y, sb_d, st_y, st_d,
    rh_y, rf_y, rx_y, rh_d, rf_d, rx_d, rq_d,
    act, dpre, acc_a, acc_b,
    ssem, rsem, lsem,
):
    bf, f32 = jnp.bfloat16, jnp.float32
    me = lax.axis_index("dp")
    ex = lax.axis_index("expert")
    xl, y, core = me // 8, (me // 2) % 4, me % 2
    z, xh = ex // 2, ex % 2

    def dev(xl, y, core):
        return xl * 8 + y * 2 + core

    y_up = (dev(xl, (y + 1) % 4, core), ex)
    y_dn = (dev(xl, (y + 3) % 4, core), ex)
    x_nb = (dev(1 - xl, y, core), ex)
    twin = (dev(xl, y, 1 - core), ex)

    def slot_peer(dz, f):
        xl2 = (1 - xl) if f else xl
        xh2 = (1 - xh) if f else xh
        return (dev(xl2, y, core), ((z + dz) % 8) * 2 + xh2)

    bar = pltpu.get_barrier_semaphore()
    everyone = [slot_peer(*s) for s in SLOTS[:0:-1]] + [y_up, y_dn, x_nb, twin]
    for peer in everyone:
        pl.semaphore_signal(bar, inc=1, device_id=peer, device_id_type=MESH)

    load = [pltpu.make_async_copy(rows_hbm.at[pl.ds(64, 16), pl.ds(0, 128)], assign_ref, lsem.at[0])]
    for n in range(16):
        src = rows_hbm.at[pl.ds(n // 8 * 32, 32), pl.ds(n % 8 * PART, PART)]
        dst = stack.at[n // 8, pl.ds(n % 8 * 32, 32), :]
        load.append(pltpu.make_async_copy(src, dst, lsem.at[1 + n]))
    w1 = pltpu.make_async_copy(win_hbm.at[0], win, lsem.at[17])
    w2 = pltpu.make_async_copy(wout_hbm.at[0], wout, lsem.at[18])
    for copy in load + [w1, w2]:
        copy.start()

    count = [0]
    started = []

    def remote(src, dst, peer):
        i = count[0]
        count[0] += 1
        copy = pltpu.make_async_remote_copy(
            src_ref=src, dst_ref=dst, send_sem=ssem.at[i], recv_sem=rsem.at[i],
            device_id=peer, device_id_type=MESH,
        )
        copy.start()
        started.append(Sent(copy))
        return started[-1]

    def dot(a, b):
        return jnp.dot(a, b, preferred_element_type=f32)

    def dot_t(a, b):
        return lax.dot_general(a, b, (((1,), (1,)), ((), ())), preferred_element_type=f32)

    def dot_l(a, b):
        return lax.dot_general(a, b, (((0,), (0,)), ((), ())), preferred_element_type=f32)

    def iota(shape, dim):
        return lax.broadcasted_iota(jnp.int32, shape, dim)

    for copy in load:
        copy.wait()
    spread = jnp.where(iota((128, 256), 0) == iota((128, 256), 1) // 8, 1.0, 0.0).astype(bf)
    order = dot(assign_ref[...], spread)[0:1, :]
    row, col = iota((256, 256), 0), iota((256, 256), 1)
    hit = ((row // 32) == (col % 8)) & ((row % 32).astype(f32) == order)
    taken = jnp.where(hit, 1.0, 0.0).astype(bf)

    for n in range(2):
        a_send[n] = dot_l(taken, stack[n]).astype(bf).reshape(EXPERTS, 16, PART)
        a_recv[n, 0] = a_send[n, ex]

    o, i = iota((128, 128), 0), iota((128, 128), 1)
    same = (o // 16 == i % 8) & ((o % 16) // 2 == i // 16) & (o % 2 == (i % 16) // 8)
    unfold = jnp.where(same, 1.0, 0.0).astype(bf)

    pl.semaphore_wait(bar, len(everyone))

    deal = {}

    def deal_out(k, n):
        for j in range(8 * k, 8 * k + 8):
            if j:
                peer = slot_peer(*SLOTS[j])
                deal[n, j] = remote(a_send.at[n, peer[1]], a_recv.at[n, j], peer)

    def rows(k, s, dx, dy):
        return pl.ds(k * 256 + s * 128 + (dx * 4 + dy) * 16, 16)

    def block(dx, dy):
        return pl.ds((dx * 4 + dy) * 16, 16)

    def span(cols):
        return pl.ds(*cols)

    class Gather:
        def __init__(self, k):
            self.k = k
            self.got = {}
            self.twins = {True: [], False: []}

        def send(self, ref, src, dst, peer, cols=(0, D)):
            a, b = rows(self.k, 0, *src), rows(self.k, 0, *dst)
            copy = remote(ref.at[a, span(cols)], ref.at[b, span(cols)], peer)
            self.got.setdefault((ref is xg, dst), []).append(copy)

        def wait(self, ref, dst):
            for copy in self.got[ref is xg, dst]:
                copy.wait_recv()

        def share(self, ref, pos):
            a, b = rows(self.k, 0, *pos), rows(self.k, 1, *pos)
            self.twins[ref is xg].append(remote(ref.at[a, :], ref.at[b, :], twin))

        def round_y(self, ref, dx):
            self.send(ref, (dx, 0), (dx, 3), y_up)
            self.send(ref, (dx, 0), (dx, 1), y_dn)

        def arrive(self, n):
            k = self.k
            for j in range(8 * k, 8 * k + 8):
                if j:
                    deal[n, j].wait_recv()
            flat = a_recv[n, pl.ds(8 * k, 8)].reshape(128, PART)
            flat = dot(unfold, flat).astype(bf)
            ref = (xg, gg)[n]
            for c in range(8):
                ref[rows(k, 0, 0, 0), pl.ds(c * PART, PART)] = flat[c * 16:(c + 1) * 16]
            if n == 0:
                self.send(xg, (0, 0), (1, 0), x_nb)
                self.round_y(xg, 0)
            else:
                self.round_y(gg, 0)
                self.send(gg, (0, 0), (1, 0), x_nb)
            self.share(ref, (0, 0))

        def take(self, ref, dx, dy):
            self.wait(ref, (dx, dy))
            side = ref is gg and dx == 1
            if dy == 3:
                self.send(ref, (dx, 3), (dx, 2), y_up, FIRST if side else LOW)
            elif dy == 1:
                self.send(ref, (dx, 1), (dx, 2), y_dn, LAST if side else HIGH)
            if ref is gg and dx == 0 and dy:
                self.send(gg, (0, dy), (1, dy), x_nb, MIDDLE if dy == 2 else (0, D))
            if ref is xg and dx == 1 and dy == 0:
                self.round_y(xg, 1)
            self.share(ref, (dx, dy))

        def whole(self, ref):
            for copy in self.twins[ref is xg]:
                copy.wait_recv()

    def chunk(k):
        return pl.ds(k * 256, 256)

    def hidden_x(k):
        acc_a[...] = jnp.zeros_like(acc_a)

        @pl.loop(0, D // WIDE)
        def _(n):
            cols = pl.ds(pl.multiple_of(n * WIDE, WIDE), WIDE)
            acc_a[...] += dot(xg[chunk(k), cols], win[cols, :])

    def hidden_g(k):
        acc_b[...] = jnp.zeros_like(acc_b)

        @pl.loop(0, D // WIDE)
        def _(n):
            cols = pl.ds(pl.multiple_of(n * WIDE, WIDE), WIDE)
            acc_b[...] += dot_t(gg[chunk(k), cols], wout[:, cols])

        pre = acc_a[...]
        sig = jax.nn.sigmoid(pre)
        act[chunk(k), :] = (pre * sig).astype(bf)
        dpre[chunk(k), :] = (acc_b[...] * (sig * (1.0 + pre * (1.0 - sig)))).astype(bf)

    class Reduce:
        def __init__(self, k, own, far, sb, st, rh, rf):
            self.k, self.own, self.far, self.sb, self.st = k, own, far, sb, st
            self.rh, self.rf = rh, rf
            self.pair = []
            self.half = {}
            self.full = {}

        def make(self, h, product):
            k = self.k

            @pl.loop(0, 4)
            def _(n):
                cols = pl.ds(pl.multiple_of(h * 2048 + n * TILE, TILE), TILE)
                t = product(k, cols)
                self.own[k, :, cols] = t[:128]
                self.far[k, :, cols] = t[128:].astype(bf)

            cols = span((LOW, HIGH)[h])
            self.pair.append(remote(self.far.at[k, :, cols], self.sb.at[k, :, cols], twin))

        def total(self, dst, dx, dy, cols, *others):
            @pl.loop(0, cols[1] // WIDE)
            def _(n):
                at = pl.ds(pl.multiple_of(cols[0] + n * WIDE, WIDE), WIDE)
                t = self.own[self.k, block(dx, dy), at] + self.sb[self.k, block(dx, dy), at].astype(f32)
                for other in others:
                    t = t + other[:, at].astype(f32)
                dst[:, at] = t.astype(bf)

        def stage(self, dx, dy):
            return self.st.at[self.k, dx * 4 + dy]

        def twins(self):
            for copy in self.pair:
                copy.wait_recv()

        def send_far(self, dx):
            self.twins()
            extra = (rx_d.at[self.k, 2],) if self is d[self.k] else ()
            if extra:
                cross[self.k, 2].wait_recv()
            st = self.stage(dx, 2)
            if extra:
                self.total(st, dx, 2, FIRST)
                self.total(st, dx, 2, MIDDLE, *extra)
                self.total(st, dx, 2, LAST)
            else:
                self.total(st, dx, 2, (0, D))
            for h, cols, peer in ((0, LOW, y_up), (1, HIGH, y_dn)):
                self.half[dx, h] = remote(st.at[:, span(cols)], self.rh.at[self.k, dx, :, span(cols)], peer)

        def send_near(self, dx, h):
            dy = (1, 3)[h]
            extra = ()
            if self is d[self.k]:
                cross[self.k, dy].wait_recv()
                extra = (rx_d.at[self.k, dy],)
            self.half[dx, h].wait_recv()
            st = self.stage(dx, dy)
            self.total(st, dx, dy, (LOW, HIGH)[h], self.rh.at[self.k, dx], *extra)
            self.total(st, dx, dy, (LOW, HIGH)[1 - h], *extra)
            self.full[dx, h] = remote(st, self.rf.at[self.k, dx, h], (y_up, y_dn)[h])

        def last(self, dx, *extra):
            for h in range(2):
                self.full[dx, h].wait_recv()
            f = self.rf
            self.total(self.stage(dx, 0), dx, 0, (0, D), f.at[self.k, dx, 0], f.at[self.k, dx, 1], *extra)

    cross, side, back = {}, {}, ([], [])

    def y_product(k, cols):
        return dot(act[chunk(k), :], wout[:, cols])

    def d_product(k, cols):
        return dot_t(dpre[chunk(k), :], win[cols, :])

    def d_cross(k, dy):
        r = d[k]
        r.twins()
        st = r.stage(1, dy)
        if dy == 2:
            r.total(st, 1, 2, (0, D))
            cross[k, 2] = remote(st.at[:, span(MIDDLE)], rx_d.at[k, 2, :, span(MIDDLE)], x_nb)
            for h, cols, peer in ((0, FIRST, y_dn), (1, LAST, y_up)):
                side[k, h] = remote(st.at[:, span(cols)], rq_d.at[k, h, :, span(cols)], peer)
            return
        if dy == 0:
            r.total(st, 1, 0, (0, D))
        elif dy == 3:
            side[k, 0].wait_recv()
            r.total(st, 1, 3, FIRST, rq_d.at[k, 0])
            r.total(st, 1, 3, MIDDLE)
            r.total(st, 1, 3, LAST)
        else:
            side[k, 1].wait_recv()
            r.total(st, 1, 1, LAST, rq_d.at[k, 1])
            r.total(st, 1, 1, FIRST)
            r.total(st, 1, 1, MIDDLE)
        cross[k, dy] = remote(st, rx_d.at[k, dy], x_nb)

    def y_cross(k):
        yy[k].last(1)
        cross[k, "y"] = remote(yy[k].stage(1, 0), rx_y.at[k], x_nb)

    def y_done(k):
        cross[k, "y"].wait_recv()
        yy[k].last(0, rx_y.at[k])

    def d_done(k):
        cross[k, 0].wait_recv()
        d[k].last(0, rx_d.at[k, 0])

    def give_back(k, n):
        parts = [(st_y, st_d)[n][k, 0, :, pl.ds(c * PART, PART)] for c in range(8)]
        flat = dot_l(unfold, jnp.concatenate(parts, axis=0)).astype(bf)
        r_send[n, pl.ds(8 * k, 8)] = flat.reshape(8, 16, PART)
        if k == 0:
            r_recv[n, ex] = r_send[n, 0]
        for j in range(8 * k, 8 * k + 8):
            if j:
                dz, f = SLOTS[j]
                back[n].append(remote(r_send.at[n, j], r_recv.at[n, ex], slot_peer(8 - dz, f)))

    def home(n, ref):
        for copy in back[n]:
            copy.wait_recv()
        flat = dot(taken, r_recv[n].reshape(256, PART)).astype(bf)
        for c in range(8):
            ref[:, pl.ds(c * PART, PART)] = flat[c * 32:(c + 1) * 32]

    def grad_out(part):
        @pl.loop(0, 2)
        def _(n):
            cols = pl.ds(pl.multiple_of(part * 1024 + n * TILE, TILE), TILE)
            gout[0, :, cols] = dot_l(act[...], gg[:, cols]).astype(bf)

    def grad_in(part):
        @pl.loop(0, 2)
        def _(n):
            cols = pl.ds(pl.multiple_of(part * 1024 + n * TILE, TILE), TILE)
            gin[0, cols, :] = dot_l(xg[:, cols], dpre[...]).astype(bf)

    def weights():
        w1.wait()
        w2.wait()

    g = [Gather(k) for k in range(2)]
    yy = [Reduce(k, own_y, far_y, sb_y, st_y, rh_y, rf_y) for k in range(2)]
    d = [Reduce(k, own_d, far_d, sb_d, st_d, rh_d, rf_d) for k in range(2)]

    step = {"w": weights, "hy": lambda: home(0, out_ref), "hd": lambda: home(1, dtok_ref)}
    for k in range(2):
        for name, call in (
            ("sx", lambda k: deal_out(k, 0)),
            ("sg", lambda k: deal_out(k, 1)),
            ("ax", lambda k: g[k].arrive(0)),
            ("ag", lambda k: g[k].arrive(1)),
            ("X", lambda k: g[k].whole(xg)),
            ("G", lambda k: g[k].whole(gg)),
            ("hx", hidden_x),
            ("hg", hidden_g),
            ("my0", lambda k: yy[k].make(0, y_product)),
            ("my1", lambda k: yy[k].make(1, y_product)),
            ("md0", lambda k: d[k].make(0, d_product)),
            ("md1", lambda k: d[k].make(1, d_product)),
            ("yf0", lambda k: yy[k].send_far(0)),
            ("yf1", lambda k: yy[k].send_far(1)),
            ("df", lambda k: d[k].send_far(0)),
            ("yn00", lambda k: yy[k].send_near(0, 0)),
            ("yn01", lambda k: yy[k].send_near(0, 1)),
            ("yn10", lambda k: yy[k].send_near(1, 0)),
            ("yn11", lambda k: yy[k].send_near(1, 1)),
            ("dn0", lambda k: d[k].send_near(0, 0)),
            ("dn1", lambda k: d[k].send_near(0, 1)),
            ("dx0", lambda k: d_cross(k, 0)),
            ("dx1", lambda k: d_cross(k, 1)),
            ("dx2", lambda k: d_cross(k, 2)),
            ("dx3", lambda k: d_cross(k, 3)),
            ("yx", y_cross),
            ("y", y_done),
            ("d", d_done),
            ("by", lambda k: give_back(k, 0)),
            ("bd", lambda k: give_back(k, 1)),
        ):
            step[name + ".%d" % k] = (lambda call, k: lambda: call(k))(call, k)
        for ref, letter in ((xg, "x"), (gg, "g")):
            for dx in range(2):
                for dy in range(4):
                    step["%s%d%d.%d" % (letter, dx, dy, k)] = (
                        lambda k, ref, dx, dy: lambda: g[k].take(ref, dx, dy)
                    )(k, ref, dx, dy)
    for part in range(4):
        step["go%d" % part] = (lambda part: lambda: grad_out(part))(part)
        step["gi%d" % part] = (lambda part: lambda: grad_in(part))(part)

    for name in ORDER:
        step[name]()
    assert count[0] == COPIES, count[0]
    for sent in started:
        sent.wait_recv()
    for sent in started:
        sent.copy.wait_send()


ORDER = (
    "sg.0", "sx.0", "ag.0", "sg.1", "ax.0", "g01.0", "sx.1", "g03.0", "x10.0", "g02.0", "ag.1", "x03.0",
    "g10.0", "x01.0", "x11.0", "g11.0", "x13.0", "g13.0", "ax.1", "x02.0", "g10.1", "w", "x12.0", "g12.0",
    "g03.1", "g01.1", "X.0", "hx.0", "x10.1", "G.0", "hg.0", "x03.1", "x01.1", "md0.0", "md1.0", "my0.0",
    "x11.1", "x13.1", "my1.0", "g02.1", "dx2.0", "g13.1", "g11.1", "x02.1", "x12.1", "yf1.0", "yf0.0",
    "dx1.0", "dx0.0", "dx3.0", "g12.1", "X.1", "hx.1", "df.0", "G.1", "hg.1", "yn10.0", "yn11.0", "my1.1",
    "my0.1", "yn01.0", "yn00.0", "md0.1", "md1.1", "yf1.1", "gi1", "yx.0", "dx2.1", "yf0.1", "yn10.1",
    "yn11.1", "dx3.1", "dx1.1", "y.0", "dn1.0", "dn0.0", "go1", "go3", "go2", "df.1", "gi0", "by.0",
    "yn00.1", "yx.1", "yn01.1", "dx0.1", "gi2", "dn1.1", "d.0", "go0", "bd.0", "dn0.1", "y.1", "by.1",
    "d.1", "bd.1", "gi3", "hy", "hd",
)

COPIES = 4 * 15 + 2 * (19 + 16 + 23)


def finish(*refs):
    sem = refs[-1]
    copies = [pltpu.make_async_copy(refs[n], refs[4 + n], sem.at[n]) for n in range(4)]
    for copy in copies:
        copy.start()
    for copy in copies:
        copy.wait()


def body(tokens, assign, w_in, w_out, cotangent):
    bf, f32 = jnp.bfloat16, jnp.float32
    order = jnp.pad(assign.astype(bf), ((0, 15), (0, D - 32)))
    rows = jnp.concatenate([tokens, cotangent, order], axis=0)
    vmem = pl.BlockSpec(memory_space=pltpu.VMEM)
    hbm = pl.BlockSpec(memory_space=pltpu.HBM)
    v = pltpu.VMEM
    shapes = tuple(jax.ShapeDtypeStruct(a.shape, bf) for a in (tokens, tokens, w_in, w_out))
    results = pl.pallas_call(
        kernel,
        out_shape=shapes,
        in_specs=[hbm] * 3,
        out_specs=(vmem,) * 4,
        scratch_shapes=[
            v((16, 128), bf), v((2, 256, PART), bf),
            v((2, EXPERTS, 16, PART), bf), v((2, EXPERTS, 16, PART), bf),
            v((2, EXPERTS, 16, PART), bf), v((2, EXPERTS, 16, PART), bf),
            v((512, D), bf), v((512, D), bf),
            v((D, HID), bf), v((HID, D), bf),
            v((2, 128, D), f32), v((2, 128, D), f32),
            v((2, 128, D), bf), v((2, 128, D), bf),
            v((2, 128, D), bf), v((2, 128, D), bf),
            v((2, 8, 16, D), bf), v((2, 8, 16, D), bf),
            v((2, 2, 16, D), bf), v((2, 2, 2, 16, D), bf), v((2, 16, D), bf),
            v((2, 1, 16, D), bf), v((2, 1, 2, 16, D), bf), v((2, 4, 16, D), bf), v((2, 2, 16, D), bf),
            v((512, HID), bf), v((512, HID), bf),
            v((256, HID), f32), v((256, HID), f32),
            pltpu.SemaphoreType.DMA((COPIES,)),
            pltpu.SemaphoreType.DMA((COPIES,)),
            pltpu.SemaphoreType.DMA((19,)),
        ],
        compiler_params=pltpu.CompilerParams(
            collective_id=0, has_side_effects=True, vmem_limit_bytes=47 * 2**20
        ),
        cost_estimate=pl.CostEstimate(
            flops=12 * 512 * D * HID, bytes_accessed=10 * 2**20, transcendentals=512 * HID
        ),
    )(rows, w_in, w_out)
    anywhere = pl.BlockSpec(memory_space=pl.ANY)
    return pl.pallas_call(
        finish,
        out_shape=shapes,
        in_specs=[anywhere] * 4,
        out_specs=(anywhere,) * 4,
        scratch_shapes=[pltpu.SemaphoreType.DMA((4,))],
        compiler_params=pltpu.CompilerParams(vmem_limit_bytes=2**20),
    )(*results)


def solution(mesh):
    in_specs = (
        P(("dp", "expert"), None),
        P(("dp", "expert"), None),
        P("expert", None, "dp"),
        P("expert", "dp", None),
        P(("dp", "expert"), None),
    )
    out_specs = (
        P(("dp", "expert"), None),
        P(("dp", "expert"), None),
        P("expert", None, "dp"),
        P("expert", "dp", None),
    )
    return jax.shard_map(body, mesh=mesh, in_specs=in_specs, out_specs=out_specs, check_vma=False)
```

```python
import jax
import jax.numpy as jnp
from jax import lax
from jax.experimental import pallas as pl
from jax.experimental.pallas import tpu as pltpu
from jax.sharding import PartitionSpec as P

MESH = pl.DeviceIdType.MESH
D = 4096
HID = 256
TILE = 512
PART = 512
WIDE = 1024
EXPERTS = 16
SLOTS = [(0, 0), (0, 1), (1, 0), (1, 1), (7, 0), (7, 1), (2, 0), (6, 1)]
SLOTS += [(3, 0), (3, 1), (5, 0), (5, 1), (4, 0), (4, 1), (2, 1), (6, 0)]
LOW, HIGH = (0, 2048), (2048, 2048)
FIRST, MIDDLE, LAST = (0, 1024), (1024, 2048), (3072, 1024)


class Sent:
    def __init__(self, copy):
        self.copy = copy
        self.due = True

    def wait_recv(self):
        if self.due:
            self.copy.wait_recv()
        self.due = False


def kernel(
    rows_hbm, win_hbm, wout_hbm,
    out_ref, dtok_ref, gin, gout,
    assign_ref, taken, stack, a_send, a_recv, r_send, r_recv,
    xg, gg, win, wout,
    own_y, own_d, far_y, far_d, sb_y, sb_d, st_y, st_d,
    rh_y, rf_y, rx_y, rh_d, rf_d, rx_d, rq_d,
    act, dpre, acc_a, acc_b,
    ssem, rsem, lsem,
):
    bf, f32 = jnp.bfloat16, jnp.float32
    me = lax.axis_index("dp")
    ex = lax.axis_index("expert")
    xl, y, core = me // 8, (me // 2) % 4, me % 2
    z, xh = ex // 2, ex % 2

    def dev(xl, y, core):
        return xl * 8 + y * 2 + core

    y_up = (dev(xl, (y + 1) % 4, core), ex)
    y_dn = (dev(xl, (y + 3) % 4, core), ex)
    x_nb = (dev(1 - xl, y, core), ex)
    twin = (dev(xl, y, 1 - core), ex)

    def slot_peer(dz, f):
        xl2 = (1 - xl) if f else xl
        xh2 = (1 - xh) if f else xh
        return (dev(xl2, y, core), ((z + dz) % 8) * 2 + xh2)

    bar = pltpu.get_barrier_semaphore()
    everyone = [slot_peer(*s) for s in SLOTS[:0:-1]] + [y_up, y_dn, x_nb, twin]
    for peer in everyone:
        pl.semaphore_signal(bar, inc=1, device_id=peer, device_id_type=MESH)

    load = [pltpu.make_async_copy(rows_hbm.at[pl.ds(64, 16), pl.ds(0, 128)], assign_ref, lsem.at[0])]
    for n in range(16):
        src = rows_hbm.at[pl.ds(n // 8 * 32, 32), pl.ds(n % 8 * PART, PART)]
        dst = stack.at[n // 8, pl.ds(n % 8 * 32, 32), :]
        load.append(pltpu.make_async_copy(src, dst, lsem.at[1 + n]))
    w1 = pltpu.make_async_copy(win_hbm.at[0], win, lsem.at[17])
    w2 = pltpu.make_async_copy(wout_hbm.at[0], wout, lsem.at[18])
    for copy in load + [w1, w2]:
        copy.start()

    count = [0]
    started = []

    def remote(src, dst, peer):
        i = count[0]
        count[0] += 1
        copy = pltpu.make_async_remote_copy(
            src_ref=src, dst_ref=dst, send_sem=ssem.at[i], recv_sem=rsem.at[i],
            device_id=peer, device_id_type=MESH,
        )
        copy.start()
        started.append(Sent(copy))
        return started[-1]

    def dot(a, b):
        return jnp.dot(a, b, preferred_element_type=f32)

    def dot_t(a, b):
        return lax.dot_general(a, b, (((1,), (1,)), ((), ())), preferred_element_type=f32)

    def dot_l(a, b):
        return lax.dot_general(a, b, (((0,), (0,)), ((), ())), preferred_element_type=f32)

    def iota(shape, dim):
        return lax.broadcasted_iota(jnp.int32, shape, dim)

    spread = jnp.where(iota((256, 128), 0) // 8 == iota((256, 128), 1), 1.0, 0.0).astype(bf)
    row, col = iota((256, 256), 0), iota((256, 256), 1)
    place = jnp.where((row & 7) == lax.shift_right_logical(col, 5), (col & 31).astype(f32), -1.0)
    o, i = iota((128, 128), 0), iota((128, 128), 1)
    same = (lax.shift_right_logical(o, 4) == (i & 7)) & ((o & 15) == lax.shift_right_logical(i, 3))
    unfold = jnp.where(same, 1.0, 0.0).astype(bf)
    load[0].wait()
    give = jnp.where(place == dot_t(spread, assign_ref[...])[:, 0:1], 1.0, 0.0).astype(bf)
    taken[...] = give

    def deal_in(n):
        for copy in load[1 + 8 * n:9 + 8 * n]:
            copy.wait()
        a_send[n] = dot(taken[...], stack[n]).astype(bf).reshape(EXPERTS, 16, PART)
        a_recv[n, 0] = a_send[n, ex]

    deal_in(0)

    pl.semaphore_wait(bar, len(everyone))

    deal = {}

    def deal_out(k, n):
        if k == 0 and n == 1:
            deal_in(1)
        for j in range(8 * k, 8 * k + 8):
            if j:
                peer = slot_peer(*SLOTS[j])
                deal[n, j] = remote(a_send.at[n, peer[1]], a_recv.at[n, j], peer)

    def rows(k, s, dx, dy):
        return pl.ds(k * 256 + s * 128 + (dx * 4 + dy) * 16, 16)

    def block(dx, dy):
        return pl.ds((dx * 4 + dy) * 16, 16)

    def span(cols):
        return pl.ds(*cols)

    class Gather:
        def __init__(self, k):
            self.k = k
            self.got = {}
            self.twins = {True: [], False: []}

        def send(self, ref, src, dst, peer, cols=(0, D)):
            a, b = rows(self.k, 0, *src), rows(self.k, 0, *dst)
            copy = remote(ref.at[a, span(cols)], ref.at[b, span(cols)], peer)
            self.got.setdefault((ref is xg, dst), []).append(copy)

        def wait(self, ref, dst):
            for copy in self.got[ref is xg, dst]:
                copy.wait_recv()

        def share(self, ref, pos):
            a, b = rows(self.k, 0, *pos), rows(self.k, 1, *pos)
            self.twins[ref is xg].append(remote(ref.at[a, :], ref.at[b, :], twin))

        def round_y(self, ref, dx):
            self.send(ref, (dx, 0), (dx, 3), y_up)
            self.send(ref, (dx, 0), (dx, 1), y_dn)

        def arrive(self, n):
            k = self.k
            for j in range(8 * k, 8 * k + 8):
                if j:
                    deal[n, j].wait_recv()
            flat = a_recv[n, pl.ds(8 * k, 8)].reshape(128, PART)
            flat = dot(unfold, flat).astype(bf)
            ref = (xg, gg)[n]
            for c in range(8):
                ref[rows(k, 0, 0, 0), pl.ds(c * PART, PART)] = flat[c * 16:(c + 1) * 16]
            if n == 0:
                self.send(xg, (0, 0), (1, 0), x_nb)
                self.round_y(xg, 0)
            else:
                self.round_y(gg, 0)
                self.send(gg, (0, 0), (1, 0), x_nb)
            self.share(ref, (0, 0))

        def take(self, ref, dx, dy):
            self.wait(ref, (dx, dy))
            side = ref is gg and dx == 1
            if dy == 3:
                self.send(ref, (dx, 3), (dx, 2), y_up, FIRST if side else LOW)
            elif dy == 1:
                self.send(ref, (dx, 1), (dx, 2), y_dn, LAST if side else HIGH)
            if ref is gg and dx == 0 and dy:
                self.send(gg, (0, dy), (1, dy), x_nb, MIDDLE if dy == 2 else (0, D))
            if ref is xg and dx == 1 and dy == 0:
                self.round_y(xg, 1)
            self.share(ref, (dx, dy))

        def whole(self, ref):
            for copy in self.twins[ref is xg]:
                copy.wait_recv()

    def chunk(k):
        return pl.ds(k * 256, 256)

    def hidden_x(k):
        acc_a[...] = jnp.zeros_like(acc_a)

        @pl.loop(0, D // WIDE)
        def _(n):
            cols = pl.ds(pl.multiple_of(n * WIDE, WIDE), WIDE)
            acc_a[...] += dot(xg[chunk(k), cols], win[cols, :])

    def hidden_g(k):
        acc_b[...] = jnp.zeros_like(acc_b)

        @pl.loop(0, D // WIDE)
        def _(n):
            cols = pl.ds(pl.multiple_of(n * WIDE, WIDE), WIDE)
            acc_b[...] += dot_t(gg[chunk(k), cols], wout[:, cols])

        pre = acc_a[...]
        sig = jax.nn.sigmoid(pre)
        act[chunk(k), :] = (pre * sig).astype(bf)
        dpre[chunk(k), :] = (acc_b[...] * (sig * (1.0 + pre * (1.0 - sig)))).astype(bf)

    class Reduce:
        def __init__(self, k, own, far, sb, st, rh, rf):
            self.k, self.own, self.far, self.sb, self.st = k, own, far, sb, st
            self.rh, self.rf = rh, rf
            self.pair = []
            self.half = {}
            self.full = {}

        def make(self, h, product):
            k = self.k

            @pl.loop(0, 4)
            def _(n):
                cols = pl.ds(pl.multiple_of(h * 2048 + n * TILE, TILE), TILE)
                t = product(k, cols)
                self.own[k, :, cols] = t[:128]
                self.far[k, :, cols] = t[128:].astype(bf)

            cols = span((LOW, HIGH)[h])
            self.pair.append(remote(self.far.at[k, :, cols], self.sb.at[k, :, cols], twin))

        def total(self, dst, dx, dy, cols, *others):
            @pl.loop(0, cols[1] // WIDE)
            def _(n):
                at = pl.ds(pl.multiple_of(cols[0] + n * WIDE, WIDE), WIDE)
                t = self.own[self.k, block(dx, dy), at] + self.sb[self.k, block(dx, dy), at].astype(f32)
                for other in others:
                    t = t + other[:, at].astype(f32)
                dst[:, at] = t.astype(bf)

        def stage(self, dx, dy):
            return self.st.at[self.k, dx * 4 + dy]

        def twins(self):
            for copy in self.pair:
                copy.wait_recv()

        def send_far(self, dx):
            self.twins()
            extra = (rx_d.at[self.k, 2],) if self is d[self.k] else ()
            if extra:
                cross[self.k, 2].wait_recv()
            st = self.stage(dx, 2)
            if extra:
                self.total(st, dx, 2, FIRST)
                self.total(st, dx, 2, MIDDLE, *extra)
                self.total(st, dx, 2, LAST)
            else:
                self.total(st, dx, 2, (0, D))
            for h, cols, peer in ((0, LOW, y_up), (1, HIGH, y_dn)):
                self.half[dx, h] = remote(st.at[:, span(cols)], self.rh.at[self.k, dx, :, span(cols)], peer)

        def send_near(self, dx, h):
            dy = (1, 3)[h]
            extra = ()
            if self is d[self.k]:
                cross[self.k, dy].wait_recv()
                extra = (rx_d.at[self.k, dy],)
            self.half[dx, h].wait_recv()
            st = self.stage(dx, dy)
            self.total(st, dx, dy, (LOW, HIGH)[h], self.rh.at[self.k, dx], *extra)
            self.total(st, dx, dy, (LOW, HIGH)[1 - h], *extra)
            self.full[dx, h] = remote(st, self.rf.at[self.k, dx, h], (y_up, y_dn)[h])

        def last(self, dx, *extra):
            for h in range(2):
                self.full[dx, h].wait_recv()
            f = self.rf
            self.total(self.stage(dx, 0), dx, 0, (0, D), f.at[self.k, dx, 0], f.at[self.k, dx, 1], *extra)

    cross, side, back = {}, {}, ([], [])

    def y_product(k, cols):
        return dot(act[chunk(k), :], wout[:, cols])

    def d_product(k, cols):
        return dot_t(dpre[chunk(k), :], win[cols, :])

    def d_cross(k, dy):
        r = d[k]
        r.twins()
        st = r.stage(1, dy)
        if dy == 2:
            r.total(st, 1, 2, (0, D))
            cross[k, 2] = remote(st.at[:, span(MIDDLE)], rx_d.at[k, 2, :, span(MIDDLE)], x_nb)
            for h, cols, peer in ((0, FIRST, y_dn), (1, LAST, y_up)):
                side[k, h] = remote(st.at[:, span(cols)], rq_d.at[k, h, :, span(cols)], peer)
            return
        if dy == 0:
            r.total(st, 1, 0, (0, D))
        elif dy == 3:
            side[k, 0].wait_recv()
            r.total(st, 1, 3, FIRST, rq_d.at[k, 0])
            r.total(st, 1, 3, MIDDLE)
            r.total(st, 1, 3, LAST)
        else:
            side[k, 1].wait_recv()
            r.total(st, 1, 1, LAST, rq_d.at[k, 1])
            r.total(st, 1, 1, FIRST)
            r.total(st, 1, 1, MIDDLE)
        cross[k, dy] = remote(st, rx_d.at[k, dy], x_nb)

    def y_cross(k):
        yy[k].last(1)
        cross[k, "y"] = remote(yy[k].stage(1, 0), rx_y.at[k], x_nb)

    def y_done(k):
        cross[k, "y"].wait_recv()
        yy[k].last(0, rx_y.at[k])

    def d_done(k):
        cross[k, 0].wait_recv()
        d[k].last(0, rx_d.at[k, 0])

    def give_back(k, n):
        parts = [(st_y, st_d)[n][k, 0, :, pl.ds(c * PART, PART)] for c in range(8)]
        flat = dot_l(unfold, jnp.concatenate(parts, axis=0)).astype(bf)
        r_send[n, pl.ds(8 * k, 8)] = flat.reshape(8, 16, PART)
        if k == 0:
            r_recv[n, ex] = r_send[n, 0]
        for j in range(8 * k, 8 * k + 8):
            if j:
                dz, f = SLOTS[j]
                back[n].append(remote(r_send.at[n, j], r_recv.at[n, ex], slot_peer(8 - dz, f)))

    def home(n, ref):
        for copy in back[n]:
            copy.wait_recv()
        flat = dot_l(taken[...], r_recv[n].reshape(256, PART)).astype(bf)
        for c in range(8):
            ref[:, pl.ds(c * PART, PART)] = flat[c * 32:(c + 1) * 32]

    def grad_out(part):
        @pl.loop(0, 2)
        def _(n):
            cols = pl.ds(pl.multiple_of(part * 1024 + n * TILE, TILE), TILE)
            gout[0, :, cols] = dot_l(act[...], gg[:, cols]).astype(bf)

    def grad_in(part):
        @pl.loop(0, 2)
        def _(n):
            cols = pl.ds(pl.multiple_of(part * 1024 + n * TILE, TILE), TILE)
            gin[0, cols, :] = dot_l(xg[:, cols], dpre[...]).astype(bf)

    def weights():
        w1.wait()
        w2.wait()

    g = [Gather(k) for k in range(2)]
    yy = [Reduce(k, own_y, far_y, sb_y, st_y, rh_y, rf_y) for k in range(2)]
    d = [Reduce(k, own_d, far_d, sb_d, st_d, rh_d, rf_d) for k in range(2)]

    step = {"w": weights, "hy": lambda: home(0, out_ref), "hd": lambda: home(1, dtok_ref)}
    for k in range(2):
        for name, call in (
            ("sx", lambda k: deal_out(k, 0)),
            ("sg", lambda k: deal_out(k, 1)),
            ("ax", lambda k: g[k].arrive(0)),
            ("ag", lambda k: g[k].arrive(1)),
            ("X", lambda k: g[k].whole(xg)),
            ("G", lambda k: g[k].whole(gg)),
            ("hx", hidden_x),
            ("hg", hidden_g),
            ("my0", lambda k: yy[k].make(0, y_product)),
            ("my1", lambda k: yy[k].make(1, y_product)),
            ("md0", lambda k: d[k].make(0, d_product)),
            ("md1", lambda k: d[k].make(1, d_product)),
            ("yf0", lambda k: yy[k].send_far(0)),
            ("yf1", lambda k: yy[k].send_far(1)),
            ("df", lambda k: d[k].send_far(0)),
            ("yn00", lambda k: yy[k].send_near(0, 0)),
            ("yn01", lambda k: yy[k].send_near(0, 1)),
            ("yn10", lambda k: yy[k].send_near(1, 0)),
            ("yn11", lambda k: yy[k].send_near(1, 1)),
            ("dn0", lambda k: d[k].send_near(0, 0)),
            ("dn1", lambda k: d[k].send_near(0, 1)),
            ("dx0", lambda k: d_cross(k, 0)),
            ("dx1", lambda k: d_cross(k, 1)),
            ("dx2", lambda k: d_cross(k, 2)),
            ("dx3", lambda k: d_cross(k, 3)),
            ("yx", y_cross),
            ("y", y_done),
            ("d", d_done),
            ("by", lambda k: give_back(k, 0)),
            ("bd", lambda k: give_back(k, 1)),
        ):
            step[name + ".%d" % k] = (lambda call, k: lambda: call(k))(call, k)
        for ref, letter in ((xg, "x"), (gg, "g")):
            for dx in range(2):
                for dy in range(4):
                    step["%s%d%d.%d" % (letter, dx, dy, k)] = (
                        lambda k, ref, dx, dy: lambda: g[k].take(ref, dx, dy)
                    )(k, ref, dx, dy)
    for part in range(4):
        step["go%d" % part] = (lambda part: lambda: grad_out(part))(part)
        step["gi%d" % part] = (lambda part: lambda: grad_in(part))(part)

    for name in ORDER:
        step[name]()
    assert count[0] == COPIES, count[0]
    for sent in started:
        sent.wait_recv()
    for sent in started:
        sent.copy.wait_send()


ORDER = (
    "sx.0", "sg.0", "ax.0", "ag.0", "sx.1", "w", "sg.1", "x01.0", "x10.0", "g03.0", "g01.0", "ax.1",
    "x11.0", "x03.0", "g02.0", "x13.0", "g13.0", "ag.1", "g11.0", "x03.1", "x12.0", "x01.1", "x02.0",
    "x10.1", "g10.0", "X.0", "g01.1", "g12.0", "hx.0", "g03.1", "G.0", "hg.0", "my0.0", "my1.0", "x13.1",
    "x11.1", "md0.0", "g11.1", "g02.1", "md1.0", "g13.1", "yf0.0", "x12.1", "yf1.0", "x02.1", "g10.1",
    "dx0.0", "dx2.0", "g12.1", "X.1", "hx.1", "yn01.0", "yn00.0", "G.1", "hg.1", "yn10.0", "yn11.0",
    "dx3.0", "my1.1", "my0.1", "dx1.0", "md0.1", "md1.1", "yf1.1", "df.0", "yx.0", "dx2.1", "yf0.1",
    "yn11.1", "yn10.1", "dn0.0", "dx3.1", "dn1.0", "y.0", "go1", "df.1", "dx1.1", "yn01.1", "go0", "go2",
    "by.0", "yx.1", "yn00.1", "gi0", "d.0", "dn1.1", "dx0.1", "dn0.1", "bd.0", "y.1", "by.1", "gi1", "go3",
    "d.1", "bd.1", "hy", "gi3", "gi2", "hd",
)

COPIES = 4 * 15 + 2 * (19 + 16 + 23)


def finish(*refs):
    sem = refs[-1]
    copies = [pltpu.make_async_copy(refs[n], refs[4 + n], sem.at[n]) for n in range(4)]
    for copy in copies:
        copy.start()
    for copy in copies:
        copy.wait()


def body(tokens, assign, w_in, w_out, cotangent):
    bf, f32 = jnp.bfloat16, jnp.float32
    order = jnp.pad(assign.astype(bf), ((0, 15), (0, D - 32)))
    rows = jnp.concatenate([tokens, cotangent, order], axis=0)
    vmem = pl.BlockSpec(memory_space=pltpu.VMEM)
    hbm = pl.BlockSpec(memory_space=pltpu.HBM)
    v = pltpu.VMEM
    shapes = tuple(jax.ShapeDtypeStruct(a.shape, bf) for a in (tokens, tokens, w_in, w_out))
    results = pl.pallas_call(
        kernel,
        out_shape=shapes,
        in_specs=[hbm] * 3,
        out_specs=(vmem,) * 4,
        scratch_shapes=[
            v((16, 128), bf), v((256, 256), bf), v((2, 256, PART), bf),
            v((2, EXPERTS, 16, PART), bf), v((2, EXPERTS, 16, PART), bf),
            v((2, EXPERTS, 16, PART), bf), v((2, EXPERTS, 16, PART), bf),
            v((512, D), bf), v((512, D), bf),
            v((D, HID), bf), v((HID, D), bf),
            v((2, 128, D), f32), v((2, 128, D), f32),
            v((2, 128, D), bf), v((2, 128, D), bf),
            v((2, 128, D), bf), v((2, 128, D), bf),
            v((2, 8, 16, D), bf), v((2, 8, 16, D), bf),
            v((2, 2, 16, D), bf), v((2, 2, 2, 16, D), bf), v((2, 16, D), bf),
            v((2, 1, 16, D), bf), v((2, 1, 2, 16, D), bf), v((2, 4, 16, D), bf), v((2, 2, 16, D), bf),
            v((512, HID), bf), v((512, HID), bf),
            v((256, HID), f32), v((256, HID), f32),
            pltpu.SemaphoreType.DMA((COPIES,)),
            pltpu.SemaphoreType.DMA((COPIES,)),
            pltpu.SemaphoreType.DMA((19,)),
        ],
        compiler_params=pltpu.CompilerParams(
            collective_id=0, has_side_effects=True, vmem_limit_bytes=47 * 2**20
        ),
        cost_estimate=pl.CostEstimate(
            flops=12 * 512 * D * HID, bytes_accessed=10 * 2**20, transcendentals=512 * HID
        ),
    )(rows, w_in, w_out)
    anywhere = pl.BlockSpec(memory_space=pl.ANY)
    return pl.pallas_call(
        finish,
        out_shape=shapes,
        in_specs=[anywhere] * 4,
        out_specs=(anywhere,) * 4,
        scratch_shapes=[pltpu.SemaphoreType.DMA((4,))],
        compiler_params=pltpu.CompilerParams(vmem_limit_bytes=2**20),
    )(*results)


def solution(mesh):
    in_specs = (
        P(("dp", "expert"), None),
        P(("dp", "expert"), None),
        P("expert", None, "dp"),
        P("expert", "dp", None),
        P(("dp", "expert"), None),
    )
    out_specs = (
        P(("dp", "expert"), None),
        P(("dp", "expert"), None),
        P("expert", None, "dp"),
        P("expert", "dp", None),
    )
    return jax.shard_map(body, mesh=mesh, in_specs=in_specs, out_specs=out_specs, check_vma=False)
```

```python
import jax
import jax.numpy as jnp
from jax import lax
from jax.experimental import pallas as pl
from jax.experimental.pallas import tpu as pltpu
from jax.sharding import PartitionSpec as P

MESH = pl.DeviceIdType.MESH
D = 4096
HID = 256
TILE = 512
PART = 512
WIDE = 1024
EXPERTS = 16
SLOTS = [(0, 0), (0, 1), (1, 0), (1, 1), (7, 0), (7, 1), (2, 0), (6, 1)]
SLOTS += [(3, 0), (3, 1), (5, 0), (5, 1), (4, 0), (4, 1), (2, 1), (6, 0)]
LOW, HIGH = (0, 2048), (2048, 2048)
FIRST, MIDDLE, LAST = (0, 768), (768, 2560), (3328, 768)


class Sent:
    def __init__(self, copy):
        self.copy = copy
        self.due = True
        self.held = True

    def wait_recv(self):
        if self.due:
            self.copy.wait_recv()
        self.due = False

    def wait_send(self):
        if self.held:
            self.copy.wait_send()
        self.held = False


def kernel(
    rows_hbm, win_hbm, wout_hbm,
    out_ref, dtok_ref, gin, gout,
    assign_ref, taken, stack, a_send, a_recv, r_send, r_recv,
    xg, gg, win, wout,
    own_y, own_d, far_y, far_d, sb_y, sb_d, st_y, st_d,
    rh_y, rf_y, rx_y, rh_d, rf_d, rx_d, rq_d,
    act, dpre, acc_a, acc_b,
    ssem, rsem, lsem,
):
    bf, f32 = jnp.bfloat16, jnp.float32
    me = lax.axis_index("dp")
    ex = lax.axis_index("expert")
    xl, y, core = me // 8, (me // 2) % 4, me % 2
    z, xh = ex // 2, ex % 2

    def dev(xl, y, core):
        return xl * 8 + y * 2 + core

    y_up = (dev(xl, (y + 1) % 4, core), ex)
    y_dn = (dev(xl, (y + 3) % 4, core), ex)
    x_nb = (dev(1 - xl, y, core), ex)
    twin = (dev(xl, y, 1 - core), ex)

    def slot_peer(dz, f):
        xl2 = (1 - xl) if f else xl
        xh2 = (1 - xh) if f else xh
        return (dev(xl2, y, core), ((z + dz) % 8) * 2 + xh2)

    bar = pltpu.get_barrier_semaphore()
    everyone = [slot_peer(*s) for s in SLOTS[:0:-1]] + [y_up, y_dn, x_nb, twin]
    for peer in everyone:
        pl.semaphore_signal(bar, inc=1, device_id=peer, device_id_type=MESH)

    load = [pltpu.make_async_copy(rows_hbm.at[pl.ds(64, 16), pl.ds(0, 128)], assign_ref, lsem.at[0])]
    for n in range(16):
        src = rows_hbm.at[pl.ds(n // 8 * 32, 32), pl.ds(n % 8 * PART, PART)]
        dst = stack.at[n // 8, pl.ds(n % 8 * 32, 32), :]
        load.append(pltpu.make_async_copy(src, dst, lsem.at[1 + n]))
    w1 = pltpu.make_async_copy(win_hbm.at[0], win, lsem.at[17])
    w2 = pltpu.make_async_copy(wout_hbm.at[0], wout, lsem.at[18])
    for copy in load + [w1, w2]:
        copy.start()

    count = [0]
    started = []

    def remote(src, dst, peer):
        i = count[0]
        count[0] += 1
        copy = pltpu.make_async_remote_copy(
            src_ref=src, dst_ref=dst, send_sem=ssem.at[i], recv_sem=rsem.at[i],
            device_id=peer, device_id_type=MESH,
        )
        copy.start()
        started.append(Sent(copy))
        return started[-1]

    def dot(a, b):
        return jnp.dot(a, b, preferred_element_type=f32)

    def dot_t(a, b):
        return lax.dot_general(a, b, (((1,), (1,)), ((), ())), preferred_element_type=f32)

    def dot_l(a, b):
        return lax.dot_general(a, b, (((0,), (0,)), ((), ())), preferred_element_type=f32)

    def iota(shape, dim):
        return lax.broadcasted_iota(jnp.int32, shape, dim)

    spread = jnp.where(iota((256, 128), 0) // 8 == iota((256, 128), 1), 1.0, 0.0).astype(bf)
    row, col = iota((256, 256), 0), iota((256, 256), 1)
    place = jnp.where((row & 7) == lax.shift_right_logical(col, 5), (col & 31).astype(f32), -1.0)
    o, i = iota((128, 128), 0), iota((128, 128), 1)
    same = (lax.shift_right_logical(o, 4) == (i & 7)) & ((o & 15) == lax.shift_right_logical(i, 3))
    unfold = jnp.where(same, 1.0, 0.0).astype(bf)
    load[0].wait()
    give = jnp.where(place == dot_t(spread, assign_ref[...])[:, 0:1], 1.0, 0.0).astype(bf)
    taken[...] = give

    def deal_in(n):
        for copy in load[1 + 8 * n:9 + 8 * n]:
            copy.wait()
        a_send[n] = dot(taken[...], stack[n]).astype(bf).reshape(EXPERTS, 16, PART)
        a_recv[n, 0] = a_send[n, ex]

    deal_in(0)

    pl.semaphore_wait(bar, len(everyone))

    deal = {}

    def deal_out(k, n):
        if k == 0 and n == 1:
            deal_in(1)
        for j in range(8 * k, 8 * k + 8):
            if j:
                peer = slot_peer(*SLOTS[j])
                deal[n, j] = remote(a_send.at[n, peer[1]], a_recv.at[n, j], peer)

    def rows(k, s, dx, dy):
        return pl.ds(k * 256 + s * 128 + (dx * 4 + dy) * 16, 16)

    def block(dx, dy):
        return pl.ds((dx * 4 + dy) * 16, 16)

    def span(cols):
        return pl.ds(*cols)

    class Gather:
        def __init__(self, k):
            self.k = k
            self.got = {}
            self.twins = {True: [], False: []}

        def send(self, ref, src, dst, peer, cols=(0, D)):
            a, b = rows(self.k, 0, *src), rows(self.k, 0, *dst)
            copy = remote(ref.at[a, span(cols)], ref.at[b, span(cols)], peer)
            self.got.setdefault((ref is xg, dst), []).append(copy)

        def wait(self, ref, dst):
            for copy in self.got[ref is xg, dst]:
                copy.wait_recv()

        def share(self, ref, pos):
            a, b = rows(self.k, 0, *pos), rows(self.k, 1, *pos)
            self.twins[ref is xg].append(remote(ref.at[a, :], ref.at[b, :], twin))

        def round_y(self, ref, dx):
            self.send(ref, (dx, 0), (dx, 3), y_up)
            self.send(ref, (dx, 0), (dx, 1), y_dn)

        def arrive(self, n):
            k = self.k
            for j in range(8 * k, 8 * k + 8):
                if j:
                    deal[n, j].wait_recv()
            flat = a_recv[n, pl.ds(8 * k, 8)].reshape(128, PART)
            flat = dot(unfold, flat).astype(bf)
            ref = (xg, gg)[n]
            for c in range(8):
                ref[rows(k, 0, 0, 0), pl.ds(c * PART, PART)] = flat[c * 16:(c + 1) * 16]
            if n == 0:
                self.send(xg, (0, 0), (1, 0), x_nb)
                self.round_y(xg, 0)
            else:
                self.round_y(gg, 0)
                self.send(gg, (0, 0), (1, 0), x_nb)
            self.share(ref, (0, 0))

        def take(self, ref, dx, dy):
            self.wait(ref, (dx, dy))
            side = ref is gg and dx == 1
            if dy == 3:
                self.send(ref, (dx, 3), (dx, 2), y_up, FIRST if side else LOW)
            elif dy == 1:
                self.send(ref, (dx, 1), (dx, 2), y_dn, LAST if side else HIGH)
            if ref is gg and dx == 0 and dy:
                self.send(gg, (0, dy), (1, dy), x_nb, MIDDLE if dy == 2 else (0, D))
            if ref is xg and dx == 1 and dy == 0:
                self.round_y(xg, 1)
            self.share(ref, (dx, dy))

        def whole(self, ref):
            for copy in self.twins[ref is xg]:
                copy.wait_recv()

    def chunk(k):
        return pl.ds(k * 256, 256)

    def hidden_x(k):
        acc_a[...] = jnp.zeros_like(acc_a)

        @pl.loop(0, D // WIDE)
        def _(n):
            cols = pl.ds(pl.multiple_of(n * WIDE, WIDE), WIDE)
            acc_a[...] += dot(xg[chunk(k), cols], win[cols, :])

    def hidden_g(k):
        acc_b[...] = jnp.zeros_like(acc_b)

        @pl.loop(0, D // WIDE)
        def _(n):
            cols = pl.ds(pl.multiple_of(n * WIDE, WIDE), WIDE)
            acc_b[...] += dot_t(gg[chunk(k), cols], wout[:, cols])

        pre = acc_a[...]
        sig = jax.nn.sigmoid(pre)
        act[chunk(k), :] = (pre * sig).astype(bf)
        dpre[chunk(k), :] = (acc_b[...] * (sig * (1.0 + pre * (1.0 - sig)))).astype(bf)

    class Reduce:
        def __init__(self, k, own, far, sb, st, rh, rf):
            self.k, self.own, self.far, self.sb, self.st = k, own, far, sb, st
            self.rh, self.rf = rh, rf
            self.pair = []
            self.half = {}
            self.full = {}

        def make(self, h, product):
            k = self.k

            @pl.loop(0, 4)
            def _(n):
                cols = pl.ds(pl.multiple_of(h * 2048 + n * TILE, TILE), TILE)
                t = product(k, cols)
                self.own[k, :, cols] = t[:128]
                self.far[k, :, cols] = t[128:].astype(bf)

            cols = span((LOW, HIGH)[h])
            self.pair.append(remote(self.far.at[k, :, cols], self.sb.at[k, :, cols], twin))

        def total(self, dst, dx, dy, cols, *others):
            for c in range(cols[0], cols[0] + cols[1], WIDE):
                at = pl.ds(c, min(WIDE, cols[0] + cols[1] - c))
                t = self.own[self.k, block(dx, dy), at] + self.sb[self.k, block(dx, dy), at].astype(f32)
                for other in others:
                    t = t + other[:, at].astype(f32)
                dst[:, at] = t.astype(bf)

        def stage(self, dx, dy):
            return self.st.at[self.k, dx * 4 + dy]

        def twins(self):
            for copy in self.pair:
                copy.wait_recv()

        def send_far(self, dx):
            self.twins()
            extra = (rx_d.at[self.k, 2],) if self is d[self.k] else ()
            if extra:
                cross[self.k, 2].wait_recv()
            st = self.stage(dx, 2)
            if extra:
                self.total(st, dx, 2, FIRST)
                self.total(st, dx, 2, MIDDLE, *extra)
                self.total(st, dx, 2, LAST)
            else:
                self.total(st, dx, 2, (0, D))
            for h, cols, peer in ((0, LOW, y_up), (1, HIGH, y_dn)):
                self.half[dx, h] = remote(st.at[:, span(cols)], self.rh.at[self.k, dx, :, span(cols)], peer)

        def send_near(self, dx, h):
            dy = (1, 3)[h]
            extra = ()
            if self is d[self.k]:
                cross[self.k, dy].wait_recv()
                extra = (rx_d.at[self.k, dy],)
            self.half[dx, h].wait_recv()
            st = self.stage(dx, dy)
            self.total(st, dx, dy, (LOW, HIGH)[h], self.rh.at[self.k, dx], *extra)
            self.total(st, dx, dy, (LOW, HIGH)[1 - h], *extra)
            self.full[dx, h] = remote(st, self.rf.at[self.k, dx, h], (y_up, y_dn)[h])

        def last(self, dx, *extra):
            for h in range(2):
                self.full[dx, h].wait_recv()
            f = self.rf
            self.total(self.stage(dx, 0), dx, 0, (0, D), f.at[self.k, dx, 0], f.at[self.k, dx, 1], *extra)

    cross, side, back = {}, {}, ([], [])

    def y_product(k, cols):
        return dot(act[chunk(k), :], wout[:, cols])

    def d_product(k, cols):
        return dot_t(dpre[chunk(k), :], win[cols, :])

    def d_cross(k, dy):
        r = d[k]
        r.twins()
        st = r.stage(1, dy)
        if dy == 2:
            r.total(st, 1, 2, (0, D))
            cross[k, 2] = remote(st.at[:, span(MIDDLE)], rx_d.at[k, 2, :, span(MIDDLE)], x_nb)
            for h, cols, peer in ((0, FIRST, y_dn), (1, LAST, y_up)):
                side[k, h] = remote(st.at[:, span(cols)], rq_d.at[k, h, :, span(cols)], peer)
            return
        if dy == 0:
            r.total(st, 1, 0, (0, D))
        elif dy == 3:
            side[k, 0].wait_recv()
            r.total(st, 1, 3, FIRST, rq_d.at[k, 0])
            r.total(st, 1, 3, MIDDLE)
            r.total(st, 1, 3, LAST)
        else:
            side[k, 1].wait_recv()
            r.total(st, 1, 1, LAST, rq_d.at[k, 1])
            r.total(st, 1, 1, FIRST)
            r.total(st, 1, 1, MIDDLE)
        cross[k, dy] = remote(st, rx_d.at[k, dy], x_nb)

    def y_cross(k):
        yy[k].last(1)
        cross[k, "y"] = remote(yy[k].stage(1, 0), rx_y.at[k], x_nb)

    def y_done(k):
        cross[k, "y"].wait_recv()
        yy[k].last(0, rx_y.at[k])

    def d_done(k):
        cross[k, 0].wait_recv()
        d[k].last(0, rx_d.at[k, 0])

    def give_back(k, n):
        parts = [(st_y, st_d)[n][k, 0, :, pl.ds(c * PART, PART)] for c in range(8)]
        flat = dot_l(unfold, jnp.concatenate(parts, axis=0)).astype(bf)
        r_send[n, pl.ds(8 * k, 8)] = flat.reshape(8, 16, PART)
        if k == 0:
            r_recv[n, ex] = r_send[n, 0]
        for j in range(8 * k, 8 * k + 8):
            if j:
                dz, f = SLOTS[j]
                back[n].append(remote(r_send.at[n, j], r_recv.at[n, ex], slot_peer(8 - dz, f)))

    def home(n, ref):
        for sent in started:
            if sent not in back[0] and sent not in back[1]:
                sent.wait_send()
        for copy in back[n]:
            copy.wait_recv()
        flat = dot_l(taken[...], r_recv[n].reshape(256, PART)).astype(bf)
        for c in range(8):
            ref[:, pl.ds(c * PART, PART)] = flat[c * 32:(c + 1) * 32]

    def grad_out(part):
        @pl.loop(0, 2)
        def _(n):
            cols = pl.ds(pl.multiple_of(part * 1024 + n * TILE, TILE), TILE)
            gout[0, :, cols] = dot_l(act[...], gg[:, cols]).astype(bf)

    def grad_in(part):
        @pl.loop(0, 2)
        def _(n):
            cols = pl.ds(pl.multiple_of(part * 1024 + n * TILE, TILE), TILE)
            gin[0, cols, :] = dot_l(xg[:, cols], dpre[...]).astype(bf)

    def weights():
        w1.wait()
        w2.wait()

    g = [Gather(k) for k in range(2)]
    yy = [Reduce(k, own_y, far_y, sb_y, st_y, rh_y, rf_y) for k in range(2)]
    d = [Reduce(k, own_d, far_d, sb_d, st_d, rh_d, rf_d) for k in range(2)]

    step = {"w": weights, "hy": lambda: home(0, out_ref), "hd": lambda: home(1, dtok_ref)}
    for k in range(2):
        for name, call in (
            ("sx", lambda k: deal_out(k, 0)),
            ("sg", lambda k: deal_out(k, 1)),
            ("ax", lambda k: g[k].arrive(0)),
            ("ag", lambda k: g[k].arrive(1)),
            ("X", lambda k: g[k].whole(xg)),
            ("G", lambda k: g[k].whole(gg)),
            ("hx", hidden_x),
            ("hg", hidden_g),
            ("my0", lambda k: yy[k].make(0, y_product)),
            ("my1", lambda k: yy[k].make(1, y_product)),
            ("md0", lambda k: d[k].make(0, d_product)),
            ("md1", lambda k: d[k].make(1, d_product)),
            ("yf0", lambda k: yy[k].send_far(0)),
            ("yf1", lambda k: yy[k].send_far(1)),
            ("df", lambda k: d[k].send_far(0)),
            ("yn00", lambda k: yy[k].send_near(0, 0)),
            ("yn01", lambda k: yy[k].send_near(0, 1)),
            ("yn10", lambda k: yy[k].send_near(1, 0)),
            ("yn11", lambda k: yy[k].send_near(1, 1)),
            ("dn0", lambda k: d[k].send_near(0, 0)),
            ("dn1", lambda k: d[k].send_near(0, 1)),
            ("dx0", lambda k: d_cross(k, 0)),
            ("dx1", lambda k: d_cross(k, 1)),
            ("dx2", lambda k: d_cross(k, 2)),
            ("dx3", lambda k: d_cross(k, 3)),
            ("yx", y_cross),
            ("y", y_done),
            ("d", d_done),
            ("by", lambda k: give_back(k, 0)),
            ("bd", lambda k: give_back(k, 1)),
        ):
            step[name + ".%d" % k] = (lambda call, k: lambda: call(k))(call, k)
        for ref, letter in ((xg, "x"), (gg, "g")):
            for dx in range(2):
                for dy in range(4):
                    step["%s%d%d.%d" % (letter, dx, dy, k)] = (
                        lambda k, ref, dx, dy: lambda: g[k].take(ref, dx, dy)
                    )(k, ref, dx, dy)
    for part in range(4):
        step["go%d" % part] = (lambda part: lambda: grad_out(part))(part)
        step["gi%d" % part] = (lambda part: lambda: grad_in(part))(part)

    for name in ORDER:
        step[name]()
    assert count[0] == COPIES, count[0]
    for sent in started:
        sent.wait_recv()
    for sent in started:
        sent.wait_send()


ORDER = (
    "sx.0", "sg.0", "ax.0", "ag.0", "sx.1", "w", "sg.1", "x01.0", "x10.0", "g03.0", "g01.0", "ax.1",
    "x11.0", "x03.0", "g02.0", "x13.0", "g13.0", "ag.1", "g11.0", "x03.1", "x12.0", "x01.1", "x02.0",
    "x10.1", "g10.0", "X.0", "g01.1", "g12.0", "hx.0", "g03.1", "G.0", "hg.0", "my0.0", "my1.0", "x13.1",
    "x11.1", "md0.0", "g11.1", "g02.1", "md1.0", "g13.1", "yf0.0", "x12.1", "yf1.0", "x02.1", "g10.1",
    "dx0.0", "dx2.0", "g12.1", "X.1", "hx.1", "yn01.0", "yn00.0", "G.1", "hg.1", "yn10.0", "yn11.0",
    "dx3.0", "my1.1", "my0.1", "dx1.0", "md0.1", "md1.1", "yf1.1", "df.0", "yx.0", "dx2.1", "yf0.1",
    "yn11.1", "yn10.1", "dn0.0", "dx3.1", "dn1.0", "y.0", "go1", "df.1", "dx1.1", "yn01.1", "go0", "go2",
    "by.0", "yx.1", "yn00.1", "gi0", "d.0", "dn1.1", "dx0.1", "dn0.1", "bd.0", "y.1", "by.1", "gi1", "go3",
    "d.1", "bd.1", "hy", "gi3", "gi2", "hd",
)

COPIES = 4 * 15 + 2 * (19 + 16 + 23)


def finish(*refs):
    sem = refs[-1]
    copies = [pltpu.make_async_copy(refs[n], refs[4 + n], sem.at[n]) for n in range(4)]
    for copy in copies:
        copy.start()
    for copy in copies:
        copy.wait()


def body(tokens, assign, w_in, w_out, cotangent):
    bf, f32 = jnp.bfloat16, jnp.float32
    order = jnp.pad(assign.astype(bf), ((0, 15), (0, D - 32)))
    rows = jnp.concatenate([tokens, cotangent, order], axis=0)
    vmem = pl.BlockSpec(memory_space=pltpu.VMEM)
    hbm = pl.BlockSpec(memory_space=pltpu.HBM)
    v = pltpu.VMEM
    shapes = tuple(jax.ShapeDtypeStruct(a.shape, bf) for a in (tokens, tokens, w_in, w_out))
    results = pl.pallas_call(
        kernel,
        out_shape=shapes,
        in_specs=[hbm] * 3,
        out_specs=(vmem,) * 4,
        scratch_shapes=[
            v((16, 128), bf), v((256, 256), bf), v((2, 256, PART), bf),
            v((2, EXPERTS, 16, PART), bf), v((2, EXPERTS, 16, PART), bf),
            v((2, EXPERTS, 16, PART), bf), v((2, EXPERTS, 16, PART), bf),
            v((512, D), bf), v((512, D), bf),
            v((D, HID), bf), v((HID, D), bf),
            v((2, 128, D), f32), v((2, 128, D), f32),
            v((2, 128, D), bf), v((2, 128, D), bf),
            v((2, 128, D), bf), v((2, 128, D), bf),
            v((2, 8, 16, D), bf), v((2, 8, 16, D), bf),
            v((2, 2, 16, D), bf), v((2, 2, 2, 16, D), bf), v((2, 16, D), bf),
            v((2, 1, 16, D), bf), v((2, 1, 2, 16, D), bf), v((2, 4, 16, D), bf), v((2, 2, 16, D), bf),
            v((512, HID), bf), v((512, HID), bf),
            v((256, HID), f32), v((256, HID), f32),
            pltpu.SemaphoreType.DMA((COPIES,)),
            pltpu.SemaphoreType.DMA((COPIES,)),
            pltpu.SemaphoreType.DMA((19,)),
        ],
        compiler_params=pltpu.CompilerParams(
            collective_id=0, has_side_effects=True, vmem_limit_bytes=47 * 2**20
        ),
        cost_estimate=pl.CostEstimate(
            flops=12 * 512 * D * HID, bytes_accessed=10 * 2**20, transcendentals=512 * HID
        ),
    )(rows, w_in, w_out)
    anywhere = pl.BlockSpec(memory_space=pl.ANY)
    return pl.pallas_call(
        finish,
        out_shape=shapes,
        in_specs=[anywhere] * 4,
        out_specs=(anywhere,) * 4,
        scratch_shapes=[pltpu.SemaphoreType.DMA((4,))],
        compiler_params=pltpu.CompilerParams(vmem_limit_bytes=2**20),
    )(*results)


def solution(mesh):
    in_specs = (
        P(("dp", "expert"), None),
        P(("dp", "expert"), None),
        P("expert", None, "dp"),
        P("expert", "dp", None),
        P(("dp", "expert"), None),
    )
    out_specs = (
        P(("dp", "expert"), None),
        P(("dp", "expert"), None),
        P("expert", None, "dp"),
        P("expert", "dp", None),
    )
    return jax.shard_map(body, mesh=mesh, in_specs=in_specs, out_specs=out_specs, check_vma=False)
```
